32 devices in a mesh: energy: 8 (over y, x, core), dom: 4 (over z).
Axes of the slice: x: 2, y: 2, z: 4, core: 2. Of those that a mesh axis runs over, the one named last changes fastest.
Arguments:
- pivots: float32 [8, 32, 320, 320], P('energy', 'dom'), may hold values from -0.0125 to 1.4125
- lower_spikes: float32 [8, 32, 320, 320], P('energy', 'dom'), may hold values from -0.0125 to 1.0025
- upper_spikes: float32 [8, 32, 320, 320], P('energy', 'dom'), may hold values from -0.0125 to 1.0025
- potential: float32 [32, 320, 320], P('dom', 'energy'), may hold values from -0.3125 to 0.3125
- grain_of_slice: int32 [32], P('dom'), may hold values from 0 to 31
- grain_shift: float32 [32], replicated, may hold values from 0.5 to 1.5
- probes: float32 [32, 320, 128], P('dom'), may hold values from -6 to 6
- weights: float32 [8], P('energy'), may hold values from 0.5 to 2
Outputs:
- response: float32 [32, 320], P('dom', 'energy')
The draws below stay inside these ranges and needn't reach their ends.
All inputs are finite; a program needn't handle non-finite values.
Results may differ from the reference program's by a relative error of at most 0.00021.
Values sent between devices are 32-bit elements; how exact they have to be, the bound alone decides.
No kernel may reach another device: no remote copies, remote signals or barrier semaphores. Data moves between devices by JAX's collectives and lax.ppermute only.
A program may use at most 128 MiB of HBM per device.

```python
import math
import jax
import jax.numpy as jnp
from jax import lax

B = 320
PROBES = 128
GRAINS = 32
SLICES = 32
ENERGIES = 8


def make_blocks(key, lower_end, upper_end):
    diag_key, noise_key = jax.random.split(key)
    diagonal = jax.random.uniform(diag_key, (ENERGIES, SLICES, B), jnp.float32, lower_end, upper_end)
    noise_part = jnp.clip(jax.random.normal(noise_key, (ENERGIES, SLICES, B, B), jnp.float32), -4.0, 4.0)
    return noise_part * (1.0 / B) + diagonal[..., None] * jnp.eye(B, dtype=jnp.float32)


def draw_pivots(key, part):
    return make_blocks(jax.random.fold_in(key, 11), 0.6, 1.3)


def draw_lower_spikes(key, part):
    return make_blocks(jax.random.fold_in(key, 23), 0.9, 0.98)


def draw_upper_spikes(key, part):
    return make_blocks(jax.random.fold_in(key, 37), 0.9, 0.98)


def place_ends(entries, key, least, largest):
    longest = entries.shape.index(max(entries.shape))
    spots = []
    for shift in (0, 1):
        where = [jax.random.randint(jax.random.fold_in(key, axis), (), 0, length) for axis, length in enumerate(entries.shape)]
        where[longest] = (where[longest] + shift) % entries.shape[longest]
        spots.append(tuple(where))
    return entries.at[spots[0]].set(least).at[spots[1]].set(largest)


def block_scale(rng, shape, pieces, smallest, largest):
    level = 1.0
    for position, shards_of in pieces:
        steps = jax.random.uniform(jax.random.fold_in(jax.random.fold_in(rng, 6), position), (shards_of,), jnp.float32, smallest / len(pieces), largest / len(pieces))
        level = level * jnp.repeat(jnp.exp(steps), shape[position] // shards_of).reshape((-1,) + (1,) * (len(shape) - 1 - position))
    return level


def scatter_about(key, extent, scale, limit, pieces=(), kind=jnp.bfloat16):
    loudness = block_scale(key, extent, pieces, -0.22, 0.18) if pieces else 1.0
    array = jax.random.normal(key, extent, jnp.float32) * scale * loudness
    return jnp.minimum(jnp.maximum(array, -limit), limit).astype(kind)


def setup_inputs(seed: int = 0) -> dict:
    seeds = jax.random.split(jax.random.key(seed), 9)
    return {
        "pivots": draw_pivots(jax.random.fold_in(seeds[8], 71), 0),
        "lower_spikes": draw_lower_spikes(jax.random.fold_in(seeds[8], 71), 0),
        "upper_spikes": draw_upper_spikes(jax.random.fold_in(seeds[8], 71), 0),
        "potential": scatter_about(seeds[3], (SLICES, B, B), B ** -0.5, 0.3125, ((0, 4), (1, 8)), jnp.float32),
        "grain_of_slice": place_ends(jax.random.randint(seeds[4], (SLICES,), 0, GRAINS), jax.random.fold_in(seeds[4], 1), 0, GRAINS - 1).astype(jnp.int32),
        "grain_shift": jnp.clip(jax.random.uniform(seeds[5], (GRAINS,), jnp.float32, 0.5, 1.5), 0.5, 1.5),
        "probes": scatter_about(seeds[6], (SLICES, B, PROBES), 1.0, 6.0, ((0, 4),), jnp.float32),
        "weights": jnp.clip(jnp.exp(math.log(2.0) - 1.3862944 * jax.random.uniform(seeds[7], (ENERGIES,), jnp.float32) ** block_scale(seeds[7], (ENERGIES,), ((0, 8),), -0.2, 0.2)), 0.5, 2.0),
    }


HIGHEST = lax.Precision.HIGHEST


def solve(pivot_blocks, lower_blocks, upper_blocks, right_side):
    solved_pivot = jnp.einsum("sij,sjk->sik", pivot_blocks, right_side, precision=HIGHEST)

    def advance(carried, inputs_pair):
        matrix_block, given_value = inputs_pair
        carried = given_value - jnp.dot(matrix_block, carried, precision=HIGHEST)
        return carried, carried

    zero_block = jnp.zeros(right_side.shape[1:], jnp.float32)
    _, climbed = lax.scan(advance, zero_block, (lower_blocks, solved_pivot))
    _, result = lax.scan(advance, zero_block, (upper_blocks, climbed), reverse=True)
    return result


def reference(pivots, lower_spikes, upper_spikes, potential, grain_of_slice, grain_shift, probes, weights):
    grain_match = grain_of_slice[:, None] == jnp.arange(GRAINS, dtype=jnp.int32)[None, :]
    grain_scale = jnp.sum(jnp.where(grain_match, grain_shift[None, :], 0.0), axis=1)
    perturb = potential * grain_scale[:, None, None]

    def per_energy(energy_inputs):
        pivot_blocks, lower_blocks, upper_blocks, weight = energy_inputs
        first_solve = solve(pivot_blocks, lower_blocks, upper_blocks, probes)
        driven = jnp.einsum("sij,sjk->sik", perturb, first_solve, precision=HIGHEST)
        second_solve = solve(pivot_blocks, lower_blocks, upper_blocks, driven)
        return weight * jnp.sum(second_solve * probes, axis=2)

    charge_terms = lax.map(per_energy, (pivots, lower_spikes, upper_spikes, weights))
    return jnp.sum(charge_terms, axis=0) / (PROBES * ENERGIES)
```

```python
import functools

import jax
import jax.numpy as jnp
from jax import lax
from jax.experimental import pallas as pl
from jax.experimental.pallas import tpu as pltpu
from jax.sharding import PartitionSpec as P

F32 = jnp.float32
BF16 = jnp.bfloat16
HIGH = lax.Precision.HIGH


def halves(x):
    high = x.astype(BF16)
    return high, (x - high.astype(F32)).astype(BF16)


def dot(a, b):
    return jnp.dot(a, b, preferred_element_type=F32)


def product(a, x):
    width = x.shape[1]
    a_high, a_low = halves(a)
    x_high, x_low = halves(x)
    if width <= 128:
        both = jnp.concatenate([x_high, x_low], axis=1)
        out = dot(jnp.concatenate([a_high, a_low], axis=1), jnp.concatenate([both, both], axis=0))
        return out[:, :width] + out[:, width:]
    return dot(
        jnp.concatenate([a_high, a_low, a_high], axis=1),
        jnp.concatenate([x_high, x_high, x_low], axis=0),
    )


def block(rows, columns, index):
    return pl.BlockSpec((1, rows, columns), index)


def whole(shape):
    return pl.BlockSpec(shape, lambda s: (0,) * len(shape))


def params():
    return pltpu.CompilerParams(vmem_limit_bytes=48 << 20)


def cost(dots, columns, orbitals, bytes_accessed):
    return pl.CostEstimate(
        flops=int(dots * 2 * 3 * orbitals * orbitals * columns),
        bytes_accessed=int(bytes_accessed),
        transcendentals=0,
    )


def forward_kernel(pivot, lower, probe, y_out, t_out, last_y, last_t, state):
    probes = probe.shape[2]
    step = pl.program_id(0)
    given = product(pivot[0], probe[0])

    @pl.when(step == 0)
    def _():
        state[:, :probes] = given
        state[:, probes:] = -lower[0]

    @pl.when(step > 0)
    def _():
        moved = product(lower[0], state[...])
        state[:, :probes] = given - moved[:, :probes]
        state[:, probes:] = -moved[:, probes:]

    y_out[0] = state[:, :probes]
    t_out[0] = state[:, probes:]
    last_y[...] = state[:, :probes]
    last_t[...] = state[:, probes:]


def forward(pivots, lower, probes):
    slices, b, k = probes.shape
    at = lambda s: (s, 0, 0)
    return pl.pallas_call(
        forward_kernel,
        grid=(slices,),
        in_specs=[block(b, b, at), block(b, b, at), block(b, k, at)],
        out_specs=[block(b, k, at), block(b, b, at), whole((b, k)), whole((b, b))],
        out_shape=[
            jax.ShapeDtypeStruct((slices, b, k), F32),
            jax.ShapeDtypeStruct((slices, b, b), F32),
            jax.ShapeDtypeStruct((b, k), F32),
            jax.ShapeDtypeStruct((b, b), F32),
        ],
        scratch_shapes=[pltpu.VMEM((b, k + b), F32)],
        compiler_params=params(),
        cost_estimate=cost(slices, 2 * k + b, b, 4 * slices * b * (3 * b + 2 * k)),
        name="forward_local",
    )(pivots, lower, probes)


def backward_kernel(upper, y, t, x_out, w_out, s_out, first_xw, first_s, state):
    k = y.shape[2]
    b = t.shape[1]
    step = pl.program_id(0)

    @pl.when(step == 0)
    def _():
        state[:, :k] = y[0]
        state[:, k : k + b] = t[0]
        state[:, k + b :] = -upper[0]

    @pl.when(step > 0)
    def _():
        moved = product(upper[0], state[...])
        state[:, :k] = y[0] - moved[:, :k]
        state[:, k : k + b] = t[0] - moved[:, k : k + b]
        state[:, k + b :] = -moved[:, k + b :]

    x_out[0] = state[:, :k]
    w_out[0] = state[:, k : k + b]
    s_out[0] = state[:, k + b :]
    first_xw[...] = state[:, : k + b]
    first_s[...] = state[:, k + b :]


def backward(upper, y, t):
    slices, b, k = y.shape
    at = lambda s: (slices - 1 - s, 0, 0)
    return pl.pallas_call(
        backward_kernel,
        grid=(slices,),
        in_specs=[block(b, b, at), block(b, k, at), block(b, b, at)],
        out_specs=[
            block(b, k, at),
            block(b, b, at),
            block(b, b, at),
            whole((b, k + b)),
            whole((b, b)),
        ],
        out_shape=[
            jax.ShapeDtypeStruct((slices, b, k), F32),
            jax.ShapeDtypeStruct((slices, b, b), F32),
            jax.ShapeDtypeStruct((slices, b, b), F32),
            jax.ShapeDtypeStruct((b, k + b), F32),
            jax.ShapeDtypeStruct((b, b), F32),
        ],
        scratch_shapes=[pltpu.VMEM((b, k + 2 * b), F32)],
        compiler_params=params(),
        cost_estimate=cost(slices, k + 2 * b, b, 4 * slices * b * (4 * b + 2 * k)),
        name="backward_local",
    )(upper, y, t)


def drive_kernel(split_rows, me, scale, pivot, w, s, x, inflow, *rest):
    pieces, out, gathered = rest[:-2], rest[-2], rest[-1]
    step = pl.program_id(0)
    if split_rows:
        rows = pieces[0].shape[1]
        for j, piece in enumerate(pieces):
            owner = lax.bitwise_xor(me[0], j)
            gathered[pl.ds(pl.multiple_of(owner * rows, 8), rows), :] = piece[0]
        potential = gathered[...]
    else:
        potential = pieces[0][0]
    base = x[0] + product(w[0], inflow[...])
    right = jnp.concatenate([base, s[0]], axis=1)
    out[0] = product(pivot[0], product(potential * scale[step], right))


def drive(me, scale, pivots, w, s, x, inflow, pieces):
    slices, b, k = x.shape
    at = lambda i: (i, 0, 0)
    scalar = pl.BlockSpec(memory_space=pltpu.SMEM)
    rows = pieces[0].shape[1]
    return pl.pallas_call(
        functools.partial(drive_kernel, len(pieces) > 1),
        grid=(slices,),
        in_specs=[
            scalar,
            scalar,
            block(b, b, at),
            block(b, b, at),
            block(b, b, at),
            block(b, k, at),
            whole((b, k)),
        ]
        + [block(rows, b, at)] * len(pieces),
        out_specs=block(b, k + b, at),
        out_shape=jax.ShapeDtypeStruct((slices, b, k + b), F32),
        scratch_shapes=[pltpu.VMEM((b, b), F32)],
        compiler_params=params(),
        cost_estimate=cost(slices, 3 * k + 2 * b, b, 4 * slices * b * (5 * b + 2 * k)),
        name="drive_blocks",
    )(me, scale, pivots, w, s, x, inflow, *pieces)


def sweep_kernel(matrix, given, out, end, state):
    step = pl.program_id(0)

    @pl.when(step == 0)
    def _():
        state[...] = given[0]

    @pl.when(step > 0)
    def _():
        state[...] = given[0] - product(matrix[0], state[...])

    out[0] = state[...]
    end[...] = state[...]


def sweep(matrices, given, reverse):
    slices, b, n = given.shape
    at = (lambda s: (slices - 1 - s, 0, 0)) if reverse else (lambda s: (s, 0, 0))
    return pl.pallas_call(
        sweep_kernel,
        grid=(slices,),
        in_specs=[block(b, b, at), block(b, n, at)],
        out_specs=[block(b, n, at), whole((b, n))],
        out_shape=[
            jax.ShapeDtypeStruct((slices, b, n), F32),
            jax.ShapeDtypeStruct((b, n), F32),
        ],
        scratch_shapes=[pltpu.VMEM((b, n), F32)],
        compiler_params=params(),
        cost_estimate=cost(slices, n, b, 4 * slices * b * (b + 2 * n)),
        name="sweep_back" if reverse else "sweep_ahead",
    )(matrices, given)


def partial_kernel(v, w, outflow, inflow, out):
    k = out.shape[2]
    wide = v[0]
    out[0] = wide[:, :k] + product(wide[:, k:], outflow[...]) + product(w[0], inflow[...])


def partial_second(v, w, outflow, inflow):
    slices, b, n = v.shape
    k = n - b
    at = lambda s: (s, 0, 0)
    return pl.pallas_call(
        partial_kernel,
        grid=(slices,),
        in_specs=[block(b, n, at), block(b, b, at), whole((b, k)), whole((b, k))],
        out_specs=block(b, k, at),
        out_shape=jax.ShapeDtypeStruct((slices, b, k), F32),
        compiler_params=params(),
        cost_estimate=cost(slices, 2 * k, b, 4 * slices * b * (2 * b + 2 * k)),
        name="second_partial",
    )(v, w, outflow, inflow)


def charge_kernel(partial, s, outflow, probe, out):
    step = pl.program_id(0)
    second = partial[0] + product(s[0], outflow[...])
    out[pl.ds(step, 1), :] = jnp.sum((second * probe[0]).T, axis=0, keepdims=True)


def charge(partial, s, outflow, probes):
    slices, b, k = probes.shape
    at = lambda i: (i, 0, 0)
    return pl.pallas_call(
        charge_kernel,
        grid=(slices,),
        in_specs=[block(b, k, at), block(b, b, at), whole((b, k)), block(b, k, at)],
        out_specs=whole((slices, b)),
        out_shape=jax.ShapeDtypeStruct((slices, b), F32),
        compiler_params=params(),
        cost_estimate=cost(slices, k, b, 4 * slices * b * (b + 2 * k)),
        name="charge_terms",
    )(partial, s, outflow, probes)


def mm(a, b):
    return jnp.dot(a, b, precision=HIGH)


def send(x, *pairs):
    return lax.ppermute(x, "dom", list(pairs))


def gather_potential(potential):
    peers = lax.axis_size("energy")
    rows = potential.shape[1]
    if peers != 8 or rows % 8:
        return (lax.all_gather(potential, "energy", axis=1, tiled=True),)
    swap = lambda x, bits: lax.ppermute(x, "energy", [(i, i ^ bits) for i in range(peers)])
    even = [potential] + [swap(potential, bits) for bits in (2, 4, 6)]
    odd = [swap(x, 1) for x in even]
    return (even[0], odd[0], even[1], odd[1], even[2], odd[2], even[3], odd[3])


def per_device(
    pivots, lower_spikes, upper_spikes, potential, grain_of_slice, grain_shift, probes, weights
):
    pivots, lower, upper = pivots[0], lower_spikes[0], upper_spikes[0]
    k = probes.shape[2]
    energies = lax.axis_size("energy")
    me = lax.axis_index("energy").astype(jnp.int32).reshape(1)
    domain = lax.axis_index("dom")
    grain_count = grain_shift.shape[0]
    grain_match = grain_of_slice[:, None] == jnp.arange(grain_count, dtype=jnp.int32)[None, :]
    grain_scale = jnp.sum(jnp.where(grain_match, grain_shift[None, :], 0.0), axis=1)
    pieces = gather_potential(potential)

    y, t, last_y, last_t = forward(pivots, lower, probes)
    in_1 = send(last_y, (0, 1))
    x, w, s, first_xw, first_s = backward(upper, y, t)
    first_x, first_w = first_xw[:, :k], first_xw[:, k:]
    from_3 = send(first_xw, (3, 2))
    x_3, w_3 = from_3[:, :k], from_3[:, k:]
    in_2 = send(last_y + mm(last_t, in_1), (1, 2))
    out_2 = last_y + mm(last_t, in_2)
    in_3 = send(out_2, (2, 3))
    inflow = in_1 + in_2 + in_3
    base_x = first_x + mm(first_w, inflow)
    outflow_2 = x_3 + mm(w_3, out_2)
    outflow_1 = send(base_x + mm(first_s, outflow_2), (2, 1))
    outflow_0 = send(base_x + mm(first_s, outflow_1), (1, 0))
    outflow = outflow_0 + outflow_1 + outflow_2

    driven = drive(me, grain_scale, pivots, w, s, x, inflow, pieces)
    ahead, ahead_end = sweep(lower, driven, False)
    back, back_end = sweep(upper, ahead, True)

    last_y = ahead_end[:, :k] + mm(ahead_end[:, k:], outflow)
    first_x = back_end[:, :k] + mm(back_end[:, k:], outflow)
    x_3 = send(first_x, (3, 2))
    in_1 = send(last_y, (0, 1))
    in_2 = send(last_y + mm(last_t, in_1), (1, 2))
    out_2 = last_y + mm(last_t, in_2)
    in_3 = send(out_2, (2, 3))
    inflow = in_1 + in_2 + in_3
    base_x = first_x + mm(first_w, inflow)
    outflow_2 = x_3 + mm(w_3, out_2)
    outflow_1 = send(base_x + mm(first_s, outflow_2), (2, 1))
    outflow_0 = send(base_x + mm(first_s, outflow_1), (1, 0))
    last_outflow = outflow_0 + outflow_1 + outflow_2

    partial = partial_second(back, w, outflow, inflow)
    terms = charge(partial, s, last_outflow, probes) * (weights[0] / (k * energies))
    slices, b = terms.shape
    split = terms.reshape(slices, energies, b // energies).transpose(1, 0, 2)
    return jnp.sum(lax.all_to_all(split, "energy", 0, 0, tiled=True), axis=0)


def solution(mesh):
    placed = (
        P("energy", "dom", None, None),
        P("energy", "dom", None, None),
        P("energy", "dom", None, None),
        P("dom", "energy", None),
        P("dom"),
        P(),
        P("dom", None, None),
        P("energy"),
    )
    return jax.shard_map(
        per_device, mesh=mesh, in_specs=placed, out_specs=P("dom", "energy"), check_vma=False
    )
```

```python
import functools

import jax
import jax.numpy as jnp
from jax import lax
from jax.experimental import pallas as pl
from jax.experimental.pallas import tpu as pltpu
from jax.sharding import PartitionSpec as P

F32 = jnp.float32
BF16 = jnp.bfloat16
HIGH = lax.Precision.HIGH
MIB = 1 << 20


def halves(x):
    high = x.astype(BF16)
    return high, (x - high.astype(F32)).astype(BF16)


def dot(a, b):
    return jnp.dot(a, b, preferred_element_type=F32)


def left_two(a):
    return jnp.concatenate(halves(a), axis=1)


def left_three(a):
    high, low = halves(a)
    return jnp.concatenate([high, low, high], axis=1)


def apply_two(a, x):
    width = x.shape[1]
    both = jnp.concatenate(halves(x), axis=1)
    out = dot(a, jnp.concatenate([both, both], axis=0))
    return out[:, :width] + out[:, width:]


def apply_three(a, high, low):
    return dot(a, jnp.concatenate([high, high, low], axis=0))


def shapes(*entries):
    return [jax.ShapeDtypeStruct(shape, kind) for shape, kind in entries]


def params(mib):
    return pltpu.CompilerParams(vmem_limit_bytes=mib * MIB)


HBM = pl.BlockSpec(memory_space=pltpu.HBM)
VMEM = pl.BlockSpec(memory_space=pltpu.VMEM)
SMEM = pl.BlockSpec(memory_space=pltpu.SMEM)


def pinned(*entries):
    return [pltpu.VMEM(shape, kind) for shape, kind in entries]


def in_vmem(*arrays):
    return [pltpu.with_memory_space_constraint(x, pltpu.VMEM) for x in arrays]


def in_hbm(*arrays):
    return [pltpu.with_memory_space_constraint(x, pltpu.HBM) for x in arrays]


def local_kernel(
    pivot, lower, upper, probe,
    x_out, high_out, low_out, last_y, last_t, first_xw, first_x, first_w, first_s,
    d, l, u, z, left_a, left_b, given_a, given_b, h, x, high, low, sem, sem_out,
):
    n, b, k = z.shape
    kb = k + b
    wide = h.shape[2]
    lefts, givens = (left_a, left_b), (given_a, given_b)

    def load(which, i):
        src, dst = ((probe, z), (pivot, d), (lower, l), (upper, u))[which]
        return pltpu.make_async_copy(src.at[i], dst.at[i], sem.at[which, i])

    def store(which, i):
        src, dst = ((x, x_out), (high, high_out), (low, low_out))[which]
        return pltpu.make_async_copy(src.at[i], dst.at[i], sem_out.at[which, i])

    def begin(i, c):
        load(0, i).start()
        load(1, i).start()
        load(2, i).start()
        return c

    def begin_upper(i, c):
        load(3, n - 1 - i).start()
        return c

    lax.fori_loop(0, n, begin, 0)
    lax.fori_loop(0, n, begin_upper, 0)

    def arrive(i):
        load(0, i).wait()
        load(1, i).wait()
        load(2, i).wait()

    def prepare(i, slot):
        givens[slot][...] = apply_two(left_two(d[i]), z[i])
        lefts[slot][...] = left_three(l[i])

    def ahead(i, slot):
        moved = apply_three(lefts[slot][...], *halves(h[i - 1]))
        h[i, :, :k] = givens[slot][...] - moved[:, :k]
        h[i, :, k:] = -moved[:, k:]

    arrive(0)
    prepare(0, 0)
    h[0] = jnp.concatenate([given_a[...], -l[0], jnp.zeros((b, wide - kb), F32)], axis=1)
    arrive(1)
    prepare(1, 1)

    def ahead_pair(j, c):
        i = 2 * j + 1
        arrive(i + 1)
        ahead(i, 1)
        prepare(i + 1, 0)
        arrive(i + 2)
        ahead(i + 1, 0)
        prepare(i + 2, 1)
        return c

    lax.fori_loop(0, n // 2 - 1, ahead_pair, 0)

    def prepare_back(i, slot):
        lefts[slot][...] = left_three(u[i])

    def keep(i, value):
        value_high, value_low = halves(value)
        x[i] = value[:, :k]
        high[i] = value_high
        low[i] = value_low
        for which in range(3):
            store(which, i).start()

    def step_back(i, slot):
        moved = apply_three(lefts[slot][...], high[i + 1], low[i + 1])
        value = jnp.concatenate([h[i] - moved[:, :wide], -moved[:, wide:]], axis=1)
        keep(i, value)
        return value

    load(3, n - 1).wait()
    load(3, n - 2).wait()
    ahead(n - 1, 1)
    prepare_back(n - 1, 0)
    last_y[...] = h[n - 1, :, :k]
    last_t[...] = h[n - 1, :, k:kb]
    keep(n - 1, jnp.concatenate([h[n - 1, :, :kb], -u[n - 1]], axis=1))
    prepare_back(n - 2, 0)

    def back_pair(j, c):
        i = n - 2 - 2 * j
        load(3, i - 1).wait()
        step_back(i, 0)
        prepare_back(i - 1, 1)
        load(3, i - 2).wait()
        step_back(i - 1, 1)
        prepare_back(i - 2, 0)
        return c

    lax.fori_loop(0, n // 2 - 1, back_pair, 0)
    value = step_back(0, 0)
    first_xw[...] = value[:, :kb]
    first_x[...] = value[:, :k]
    first_w[...] = value[:, k:kb]
    first_s[...] = value[:, kb:]

    def drain(i, c):
        for which in range(3):
            store(which, i).wait()
        return c

    lax.fori_loop(0, n, drain, 0)


def local_maps(pivots, lower, upper, probes):
    n, b, k = probes.shape
    wide = -(-(k + b) // 128) * 128
    full = k + 2 * b
    v = pltpu.VMEM
    return pl.pallas_call(
        local_kernel,
        in_specs=[HBM] * 4,
        out_specs=[HBM] * 3 + [VMEM] * 6,
        out_shape=[
            pltpu.HBM((n, b, k), F32),
            pltpu.HBM((n, b, full), BF16),
            pltpu.HBM((n, b, full), BF16),
        ]
        + pinned(
            ((b, k), F32),
            ((b, b), F32),
            ((b, k + b), F32),
            ((b, k), F32),
            ((b, b), F32),
            ((b, b), F32),
        ),
        scratch_shapes=[
            v((n, b, b), F32),
            v((n, b, b), F32),
            v((n, b, b), F32),
            v((n, b, k), F32),
            v((b, 3 * b), BF16),
            v((b, 3 * b), BF16),
            v((b, k), F32),
            v((b, k), F32),
            v((n, b, wide), F32),
            v((n, b, k), F32),
            v((n, b, full), BF16),
            v((n, b, full), BF16),
            pltpu.SemaphoreType.DMA((4, n)),
            pltpu.SemaphoreType.DMA((3, n)),
        ],
        compiler_params=params(52),
        name="local_maps",
    )(*in_hbm(pivots, lower, upper, probes))


def drive_kernel(start, count, me, scale, pivot, lower, upper, *rest):
    pieces, rest = rest[:count], rest[count:]
    out, lower_out, upper_out, gathered = rest[-4:]
    step = pl.program_id(0) + start
    if count > 1:
        rows = pieces[0].shape[1]
        for j, piece in enumerate(pieces):
            owner = lax.bitwise_xor(me[0], j)
            gathered[pl.ds(pl.multiple_of(owner * rows, 8), rows), :] = piece[0]
        potential = gathered[...]
    else:
        potential = pieces[0][0]
    out[0] = left_two(apply_three(left_three(pivot[0]), *halves(potential * scale[step])))
    lower_out[0] = left_two(lower[0])
    upper_out[0] = left_two(upper[0])


def drive(start, stop, me, scale, pivots, lower, upper, pieces, done=()):
    n, b, _ = pivots.shape
    rows = pieces[0].shape[1]
    at = lambda i: (i + start, 0, 0)
    inputs = (me, scale, *in_hbm(pivots, lower, upper), *pieces)
    return pl.pallas_call(
        functools.partial(drive_kernel, start, len(pieces)),
        grid=(stop - start,),
        in_specs=[SMEM, SMEM]
        + [pl.BlockSpec((1, b, b), at)] * 3
        + [pl.BlockSpec((1, rows, b), at)] * len(pieces)
        + [pl.BlockSpec(memory_space=pl.ANY)] * len(done),
        out_specs=[pl.BlockSpec((1, b, 2 * b), at)] * 3,
        out_shape=pinned(*[((n, b, 2 * b), BF16)] * 3),
        scratch_shapes=[pltpu.VMEM((b, b), F32)],
        input_output_aliases={len(inputs) + i: i for i in range(len(done))},
        compiler_params=params(12),
        name="drive_maps",
    )(*inputs, *done)


def apply_maps(high, low, i, flows):
    k = flows.shape[1] // 2
    skip = high.shape[2] - flows.shape[0]
    maps = jnp.concatenate([high[i, :, skip:], low[i, :, skip:]], axis=1)
    out = dot(maps, jnp.concatenate([flows, flows], axis=0))
    return out[:, :k] + out[:, k:]


def second_kernel(
    x, high, low, driver, lower, upper, probes, inflow, outflow, out, last, first, y
):
    n, b, k = x.shape
    flows = jnp.concatenate(halves(jnp.concatenate([inflow[...], outflow[...]], axis=0)), axis=1)

    def given(i, c):
        out[i] = apply_two(driver[i], x[i] + apply_maps(high, low, i, flows))
        return c

    lax.fori_loop(0, n, given, 0)
    y[0] = out[0]

    def ahead(i, c):
        y[i] = out[i] - apply_two(lower[i], y[i - 1])
        return c

    lax.fori_loop(1, n, ahead, 0)
    last[...] = y[n - 1]
    out[n - 1] = y[n - 1]

    def back(r, c):
        i = n - 1 - r
        out[i] = y[i] - apply_two(upper[i], out[i + 1])
        return c

    lax.fori_loop(1, n, back, 0)
    first[...] = out[0]


def second(x, high, low, driver, lower, upper, probes, inflow, outflow):
    n, b, k = x.shape
    return pl.pallas_call(
        second_kernel,
        in_specs=[VMEM] * 9,
        out_specs=[VMEM] * 3,
        out_shape=pinned(((n, b, k), F32), ((b, k), F32), ((b, k), F32)),
        scratch_shapes=[pltpu.VMEM((n, b, k), F32)],
        compiler_params=params(10),
        name="second_local",
    )(*in_vmem(x, high, low, driver, lower, upper, probes), inflow, outflow)


def charge_kernel(places, weight, x, high, low, probe, in_1, in_2, out_1, out_2, ended, *outs):
    n, b, k = x.shape
    at, energy = places[0], places[1]
    none = jnp.zeros_like(ended)
    inflow = jnp.where(at == 1, in_1[...], jnp.where(at == 2, in_2[...], none))
    inflow = jnp.where(at == 3, ended[...], inflow)
    outflow = jnp.where(at == 1, out_1[...], jnp.where(at == 2, out_2[...], none))
    outflow = jnp.where(at == 0, ended[...], outflow)
    flows = jnp.concatenate(halves(jnp.concatenate([inflow, outflow], axis=0)), axis=1)
    terms = outs[-1]
    for i in range(n):
        value = x[i] + apply_maps(high, low, i, flows)
        terms[i : i + 1, :] = jnp.sum((value * probe[i]).T, axis=0, keepdims=True) * weight[0]
    if len(outs) > 1:
        blocks = outs[0]
        owners, _, rows = blocks.shape
        for owner in range(owners):
            j = lax.bitwise_xor(energy, owner)
            blocks[lax.div(j, 2) + lax.rem(j, 2) * (owners // 2)] = terms[:, owner * rows : (owner + 1) * rows]


def charge(places, weight, energies, x, high, low, probes, *flows):
    n, b, k = probes.shape
    by_swaps = energies == 8
    return pl.pallas_call(
        charge_kernel,
        in_specs=[SMEM] * 2 + [VMEM] * (4 + len(flows)),
        out_specs=VMEM,
        out_shape=pltpu.VMEM((energies, n, b // energies) if by_swaps else (n, b), F32),
        scratch_shapes=[pltpu.VMEM((n, b), F32)] if by_swaps else [],
        compiler_params=params(10),
        name="charge_terms",
    )(places, weight, *in_vmem(x, high, low, probes), *flows)


def mm(a, b):
    return jnp.dot(a, b, precision=HIGH)


def send(x, *pairs):
    return lax.ppermute(x, "dom", list(pairs))


def near(x, ways):
    peers = lax.axis_size("energy")
    return [lax.ppermute(x, "energy", [(i, i ^ way) for i in range(peers)]) for way in ways]


def together(*values):
    return lax.optimization_barrier(values)


def per_device(
    pivots, lower_spikes, upper_spikes, potential, grain_of_slice, grain_shift, probes, weights
):
    pivots, lower, upper = pivots[0], lower_spikes[0], upper_spikes[0]
    k = probes.shape[2]
    energies = lax.axis_size("energy")
    me = lax.axis_index("energy").astype(jnp.int32).reshape(1)
    domain = lax.axis_index("dom")
    grain_count = grain_shift.shape[0]
    grain_match = grain_of_slice[:, None] == jnp.arange(grain_count, dtype=jnp.int32)[None, :]
    grain_scale = jnp.sum(jnp.where(grain_match, grain_shift[None, :], 0.0), axis=1)
    by_swaps = energies == 8 and potential.shape[1] % 8 == 0

    places = jnp.stack([domain, lax.axis_index("energy")]).astype(jnp.int32)
    n, b = pivots.shape[:2]

    even = near(potential, (2, 4, 6)) if by_swaps else []
    x, high, low, last_y, last_t, first_xw, first_x, first_w, first_s = local_maps(
        pivots, lower, upper, probes
    )

    if by_swaps:
        last_y, first_xw, even[0], even[1] = together(last_y, first_xw, even[0], even[1])
    in_1 = send(last_y, (0, 1))
    from_3 = send(first_xw, (3, 2))
    if by_swaps:
        in_1, even[2] = together(in_1, even[2])
    out_1 = last_y + mm(last_t, in_1)
    in_2 = send(out_1, (1, 2))
    if by_swaps:
        even = [potential] + even
        odd = [near(block, (1,))[0] for block in even]
        pieces = [block for pair in zip(even, odd) for block in pair]
    else:
        pieces = [lax.all_gather(potential, "energy", axis=1, tiled=True)]
    out_2 = last_y + mm(last_t, in_2)
    in_3 = send(out_2, (2, 3))
    scale, _ = together(grain_scale, out_2)
    driven = drive(0, n // 2, me, scale, pivots, lower, upper, pieces)
    from_3, *driven = together(from_3, *driven)
    x_3, w_3 = from_3[:, :k], from_3[:, k:]
    inflow = in_1 + in_2 + in_3
    outflow_2 = x_3 + mm(w_3, out_2)
    turn = first_x + mm(first_w, in_1 + in_2) + mm(first_s, outflow_2)
    outflow_1 = send(turn, (2, 1))
    scale, _ = together(scale, turn)
    driven = drive(n // 2, n, me, scale, pivots, lower, upper, pieces, driven)
    outflow_1, *driven = together(outflow_1, *driven)
    outflow_0 = send(first_x + mm(first_w, in_1) + mm(first_s, outflow_1), (1, 0))
    outflow_0, w_3 = together(outflow_0, w_3)
    around = send(first_w + mm(first_s, mm(w_3, last_t)), (2, 1))
    outflow = outflow_0 + outflow_1 + outflow_2

    x, last_y, first_x = second(x, high, low, *driven, probes, inflow, outflow)

    last_y, first_x, around = together(last_y, first_x, around)
    x_3 = send(first_x, (3, 2))
    in_1 = send(last_y, (0, 1))
    joined = jnp.where(
        domain == 1,
        last_y + mm(last_t, in_1),
        first_x + mm(first_s, x_3 + mm(w_3, last_y)),
    )
    swapped = send(joined, (1, 2), (2, 1))
    own = swapped + mm(around, joined)
    out_2 = last_y + mm(last_t, swapped)
    crossing = jnp.where(
        domain == 1, first_x + mm(first_w, in_1) + mm(first_s, own), out_2
    )
    ended = send(crossing, (1, 0), (2, 3))
    out_2, _ = together(out_2, crossing)
    beyond = x_3 + mm(w_3, out_2)

    weight = weights / (k * energies)
    terms = charge(places, weight, energies, x, high, low, probes, in_1, swapped, own, beyond, ended)
    if energies == 8:
        half = energies // 2
        total = terms[:half] + near(terms[half:], (1,))[0]
        parts = [near(total[j], (2 * j,))[0] for j in range(1, half)]
        return total[0] + parts[0] + parts[1] + parts[2]
    split = terms.reshape(n, energies, b // energies).transpose(1, 0, 2)
    return jnp.sum(lax.all_to_all(split, "energy", 0, 0, tiled=True), axis=0)


def solution(mesh):
    placed = (
        P("energy", "dom", None, None),
        P("energy", "dom", None, None),
        P("energy", "dom", None, None),
        P("dom", "energy", None),
        P("dom"),
        P(),
        P("dom", None, None),
        P("energy"),
    )
    return jax.shard_map(
        per_device, mesh=mesh, in_specs=placed, out_specs=P("dom", "energy"), check_vma=False
    )
```

```python
import jax
import jax.numpy as jnp
from jax import lax
from jax.experimental import pallas as pl
from jax.experimental.pallas import tpu as pltpu
from jax.sharding import PartitionSpec as P

F32 = jnp.float32
BF16 = jnp.bfloat16
HIGH = lax.Precision.HIGH
MIB = 1 << 20


def halves(x):
    high = x.astype(BF16)
    return high, (x - high.astype(F32)).astype(BF16)


def dot(a, b):
    return jnp.dot(a, b, preferred_element_type=F32)


def left_two(a):
    return jnp.concatenate(halves(a), axis=1)


def left_three(a):
    high, low = halves(a)
    return jnp.concatenate([high, low, high], axis=1)


def apply_two(a, x):
    width = x.shape[1]
    both = jnp.concatenate(halves(x), axis=1)
    out = dot(a, jnp.concatenate([both, both], axis=0))
    return out[:, :width] + out[:, width:]


def apply_three(a, high, low):
    return dot(a, jnp.concatenate([high, high, low], axis=0))


def shapes(*entries):
    return [jax.ShapeDtypeStruct(shape, kind) for shape, kind in entries]


def cost(us):
    return pl.CostEstimate(flops=int(us * 1e9), bytes_accessed=0, transcendentals=0)


def params(mib):
    return pltpu.CompilerParams(vmem_limit_bytes=mib * MIB)


HBM = pl.BlockSpec(memory_space=pltpu.HBM)
VMEM = pl.BlockSpec(memory_space=pltpu.VMEM)
SMEM = pl.BlockSpec(memory_space=pltpu.SMEM)


def pinned(*entries):
    return [pltpu.VMEM(shape, kind) for shape, kind in entries]


def in_vmem(*arrays):
    return [pltpu.with_memory_space_constraint(x, pltpu.VMEM) for x in arrays]


def in_hbm(*arrays):
    return [pltpu.with_memory_space_constraint(x, pltpu.HBM) for x in arrays]


def local_kernel(
    pivot, lower, upper, probe,
    x_out, high_out, low_out, last_y, last_t, first_xw, first_x, first_w, first_s,
    d, l, u, z, left_a, left_b, given_a, given_b, h, x, high, low, sem, sem_out,
):
    n, b, k = z.shape
    kb = k + b
    wide = h.shape[2]
    lefts, givens = (left_a, left_b), (given_a, given_b)

    def load(which, i):
        src, dst = ((probe, z), (pivot, d), (lower, l), (upper, u))[which]
        return pltpu.make_async_copy(src.at[i], dst.at[i], sem.at[which, i])

    def store(which, i):
        src, dst = ((x, x_out), (high, high_out), (low, low_out))[which]
        return pltpu.make_async_copy(src.at[i], dst.at[i], sem_out.at[which, i])

    def begin(i, c):
        load(0, i).start()
        load(1, i).start()
        load(2, i).start()
        return c

    def begin_upper(i, c):
        load(3, n - 1 - i).start()
        return c

    lax.fori_loop(0, n, begin, 0)
    lax.fori_loop(0, n, begin_upper, 0)

    def arrive(i):
        load(0, i).wait()
        load(1, i).wait()
        load(2, i).wait()

    def prepare(i, slot):
        givens[slot][...] = apply_two(left_two(d[i]), z[i])
        lefts[slot][...] = left_three(l[i])

    def ahead(i, slot):
        moved = apply_three(lefts[slot][...], *halves(h[i - 1]))
        h[i, :, :k] = givens[slot][...] - moved[:, :k]
        h[i, :, k:] = -moved[:, k:]

    arrive(0)
    prepare(0, 0)
    h[0] = jnp.concatenate([given_a[...], -l[0], jnp.zeros((b, wide - kb), F32)], axis=1)
    arrive(1)
    prepare(1, 1)

    def ahead_pair(j, c):
        i = 2 * j + 1
        arrive(i + 1)
        ahead(i, 1)
        prepare(i + 1, 0)
        arrive(i + 2)
        ahead(i + 1, 0)
        prepare(i + 2, 1)
        return c

    lax.fori_loop(0, n // 2 - 1, ahead_pair, 0)

    def prepare_back(i, slot):
        lefts[slot][...] = left_three(u[i])

    def keep(i, value):
        value_high, value_low = halves(value)
        x[i] = value[:, :k]
        high[i] = value_high
        low[i] = value_low
        for which in range(3):
            store(which, i).start()

    def step_back(i, slot):
        moved = apply_three(lefts[slot][...], high[i + 1], low[i + 1])
        value = jnp.concatenate([h[i] - moved[:, :wide], -moved[:, wide:]], axis=1)
        keep(i, value)
        return value

    load(3, n - 1).wait()
    load(3, n - 2).wait()
    ahead(n - 1, 1)
    prepare_back(n - 1, 0)
    last_y[...] = h[n - 1, :, :k]
    last_t[...] = h[n - 1, :, k:kb]
    keep(n - 1, jnp.concatenate([h[n - 1, :, :kb], -u[n - 1]], axis=1))
    prepare_back(n - 2, 0)

    def back_pair(j, c):
        i = n - 2 - 2 * j
        load(3, i - 1).wait()
        step_back(i, 0)
        prepare_back(i - 1, 1)
        load(3, i - 2).wait()
        step_back(i - 1, 1)
        prepare_back(i - 2, 0)
        return c

    lax.fori_loop(0, n // 2 - 1, back_pair, 0)
    value = step_back(0, 0)
    first_xw[...] = value[:, :kb]
    first_x[...] = value[:, :k]
    first_w[...] = value[:, k:kb]
    first_s[...] = value[:, kb:]

    def drain(i, c):
        for which in range(3):
            store(which, i).wait()
        return c

    lax.fori_loop(0, n, drain, 0)


def local_maps(pivots, lower, upper, probes):
    n, b, k = probes.shape
    wide = -(-(k + b) // 128) * 128
    full = k + 2 * b
    v = pltpu.VMEM
    return pl.pallas_call(
        local_kernel,
        in_specs=[HBM] * 4,
        out_specs=[HBM] * 3 + [VMEM] * 6,
        out_shape=[
            pltpu.HBM((n, b, k), F32),
            pltpu.HBM((n, b, full), BF16),
            pltpu.HBM((n, b, full), BF16),
        ]
        + pinned(
            ((b, k), F32),
            ((b, b), F32),
            ((b, k + b), F32),
            ((b, k), F32),
            ((b, b), F32),
            ((b, b), F32),
        ),
        scratch_shapes=[
            v((n, b, b), F32),
            v((n, b, b), F32),
            v((n, b, b), F32),
            v((n, b, k), F32),
            v((b, 3 * b), BF16),
            v((b, 3 * b), BF16),
            v((b, k), F32),
            v((b, k), F32),
            v((n, b, wide), F32),
            v((n, b, k), F32),
            v((n, b, full), BF16),
            v((n, b, full), BF16),
            pltpu.SemaphoreType.DMA((4, n)),
            pltpu.SemaphoreType.DMA((3, n)),
        ],
        compiler_params=params(52),
        cost_estimate=cost(15),
        name="local_maps",
    )(*in_hbm(pivots, lower, upper, probes))


def drive_kernel(me, scale, pivot, *rest):
    pieces, out, gathered = rest[:-2], rest[-2], rest[-1]
    step = pl.program_id(0)
    if len(pieces) > 1:
        rows = pieces[0].shape[1]
        for j, piece in enumerate(pieces):
            owner = lax.bitwise_xor(me[0], j)
            gathered[pl.ds(pl.multiple_of(owner * rows, 8), rows), :] = piece[0]
        potential = gathered[...]
    else:
        potential = pieces[0][0]
    out[step] = left_two(apply_three(left_three(pivot[0]), *halves(potential * scale[step])))


def drive(me, scale, pivots, pieces):
    n, b, _ = pivots.shape
    rows = pieces[0].shape[1]
    at = lambda i: (i, 0, 0)
    return pl.pallas_call(
        drive_kernel,
        grid=(n,),
        in_specs=[SMEM, SMEM, pl.BlockSpec((1, b, b), at)]
        + [pl.BlockSpec((1, rows, b), at)] * len(pieces),
        out_specs=VMEM,
        out_shape=pltpu.VMEM((n, b, 2 * b), BF16),
        scratch_shapes=[pltpu.VMEM((b, b), F32)],
        compiler_params=params(10),
        cost_estimate=cost(0.01),
        name="drive_maps",
    )(me, scale, *in_hbm(pivots, *pieces))


def apply_maps(high, low, i, flows):
    k = flows.shape[1] // 2
    skip = high.shape[2] - flows.shape[0]
    maps = jnp.concatenate([high[i, :, skip:], low[i, :, skip:]], axis=1)
    out = dot(maps, jnp.concatenate([flows, flows], axis=0))
    return out[:, :k] + out[:, k:]


def second_ahead_kernel(
    lower, upper, x, high, low, driver, probes, in_1, in_2, in_3, out_0, out_1, out_2,
    y, last, left_u, l, u, left_l, out, sem,
):
    n, b, k = x.shape
    load_l = lambda i: pltpu.make_async_copy(lower.at[i], l.at[i], sem.at[0, i])
    load_u = lambda i: pltpu.make_async_copy(upper.at[i], u.at[i], sem.at[1, i])

    def begin(i, c):
        load_l(i).start()
        load_u(i).start()
        return c

    lax.fori_loop(0, n, begin, 0)
    inflow = in_1[...] + in_2[...] + in_3[...]
    outflow = out_0[...] + out_1[...] + out_2[...]
    flows = jnp.concatenate(halves(jnp.concatenate([inflow, outflow], axis=0)), axis=1)

    def given(i, c):
        load_l(i).wait()
        load_u(i).wait()
        out[i] = apply_two(driver[i], x[i] + apply_maps(high, low, i, flows))
        left_l[i] = left_two(l[i])
        left_u[i] = left_two(u[i])
        return c

    lax.fori_loop(0, n, given, 0)
    y[0] = out[0]

    def ahead(i, c):
        y[i] = out[i] - apply_two(left_l[i], y[i - 1])
        return c

    lax.fori_loop(1, n, ahead, 0)
    last[...] = y[n - 1]


def second_ahead(lower, upper, x, high, low, driver, probes, *flows):
    n, b, k = x.shape
    return pl.pallas_call(
        second_ahead_kernel,
        in_specs=[HBM] * 2 + [VMEM] * (5 + len(flows)),
        out_specs=[VMEM] * 3,
        out_shape=pinned(((n, b, k), F32), ((b, k), F32), ((n, b, 2 * b), BF16)),
        scratch_shapes=[
            pltpu.VMEM((n, b, b), F32),
            pltpu.VMEM((n, b, b), F32),
            pltpu.VMEM((n, b, 2 * b), BF16),
            pltpu.VMEM((n, b, k), F32),
            pltpu.SemaphoreType.DMA((2, n)),
        ],
        compiler_params=params(18),
        cost_estimate=cost(9),
        name="second_ahead",
    )(*in_hbm(lower, upper), *in_vmem(x, high, low, driver, probes), *flows)


def second_back_kernel(y, left_u, x_out, first, out, sem):
    n = y.shape[0]
    store = lambda i: pltpu.make_async_copy(out.at[i], x_out.at[i], sem.at[i])
    out[n - 1] = y[n - 1]
    store(n - 1).start()

    def back(r, c):
        i = n - 1 - r
        out[i] = y[i] - apply_two(left_u[i], out[i + 1])
        store(i).start()
        return c

    lax.fori_loop(1, n, back, 0)
    first[...] = out[0]

    def drain(i, c):
        store(i).wait()
        return c

    lax.fori_loop(0, n, drain, 0)


def second_back(y, left_u):
    n, b, k = y.shape
    return pl.pallas_call(
        second_back_kernel,
        in_specs=[VMEM] * 2,
        out_specs=[HBM, VMEM],
        out_shape=[pltpu.HBM((n, b, k), F32), pltpu.VMEM((b, k), F32)],
        scratch_shapes=[pltpu.VMEM((n, b, k), F32), pltpu.SemaphoreType.DMA((n,))],
        compiler_params=params(4),
        cost_estimate=cost(4),
        name="second_back",
    )(*in_vmem(y, left_u))


def charge_kernel(places, weight, x, high, low, probe, in_1, in_2, out_1, out_2, ended, *outs):
    n, b, k = x.shape
    at, energy = places[0], places[1]
    none = jnp.zeros_like(ended)
    inflow = jnp.where(at == 1, in_1[...], jnp.where(at == 2, in_2[...], none))
    inflow = jnp.where(at == 3, ended[...], inflow)
    outflow = jnp.where(at == 1, out_1[...], jnp.where(at == 2, out_2[...], none))
    outflow = jnp.where(at == 0, ended[...], outflow)
    flows = jnp.concatenate(halves(jnp.concatenate([inflow, outflow], axis=0)), axis=1)
    terms = outs[-1]
    for i in range(n):
        value = x[i] + apply_maps(high, low, i, flows)
        terms[i : i + 1, :] = jnp.sum((value * probe[i]).T, axis=0, keepdims=True) * weight[0]
    if len(outs) > 1:
        blocks = outs[0]
        owners, _, rows = blocks.shape
        for owner in range(owners):
            j = lax.bitwise_xor(energy, owner)
            blocks[lax.div(j, 2) + lax.rem(j, 2) * (owners // 2)] = terms[:, owner * rows : (owner + 1) * rows]


def charge(places, weight, energies, x, high, low, probes, *flows):
    n, b, k = probes.shape
    by_swaps = energies == 8
    return pl.pallas_call(
        charge_kernel,
        in_specs=[SMEM] * 2 + [VMEM] * (4 + len(flows)),
        out_specs=VMEM,
        out_shape=pltpu.VMEM((energies, n, b // energies) if by_swaps else (n, b), F32),
        scratch_shapes=[pltpu.VMEM((n, b), F32)] if by_swaps else [],
        compiler_params=params(10),
        name="charge_terms",
    )(places, weight, *in_vmem(x, high, low, probes), *flows)


def mm(a, b):
    return jnp.dot(a, b, precision=HIGH)


def send(x, *pairs):
    return lax.ppermute(x, "dom", list(pairs))


def near(x, ways):
    peers = lax.axis_size("energy")
    return [lax.ppermute(x, "energy", [(i, i ^ way) for i in range(peers)]) for way in ways]


def together(*values):
    return lax.optimization_barrier(values)


def per_device(
    pivots, lower_spikes, upper_spikes, potential, grain_of_slice, grain_shift, probes, weights
):
    pivots, lower, upper = pivots[0], lower_spikes[0], upper_spikes[0]
    k = probes.shape[2]
    energies = lax.axis_size("energy")
    me = lax.axis_index("energy").astype(jnp.int32).reshape(1)
    domain = lax.axis_index("dom")
    grain_count = grain_shift.shape[0]
    grain_match = grain_of_slice[:, None] == jnp.arange(grain_count, dtype=jnp.int32)[None, :]
    grain_scale = jnp.sum(jnp.where(grain_match, grain_shift[None, :], 0.0), axis=1)
    by_swaps = energies == 8 and potential.shape[1] % 8 == 0

    places = jnp.stack([domain, lax.axis_index("energy")]).astype(jnp.int32)
    n, b = pivots.shape[:2]

    even = near(potential, (2, 4, 6)) if by_swaps else []
    x, high, low, last_y, last_t, first_xw, first_x, first_w, first_s = local_maps(
        pivots, lower, upper, probes
    )

    in_1 = send(last_y, (0, 1))
    from_3 = send(first_xw, (3, 2))
    if by_swaps:
        in_1, *even = together(in_1, *even)
    out_1 = last_y + mm(last_t, in_1)
    in_2 = send(out_1, (1, 2))
    if by_swaps:
        even = [potential] + even
        odd = [near(block, (1,))[0] for block in even]
        pieces = [block for pair in zip(even, odd) for block in pair]
    else:
        pieces = [lax.all_gather(potential, "energy", axis=1, tiled=True)]
    driver = drive(me, grain_scale, pivots, pieces)
    in_2, from_3, driver = together(in_2, from_3, driver)
    out_2 = last_y + mm(last_t, in_2)
    base = first_x + mm(first_w, in_1 + in_2)
    outflow_2 = from_3[:, :k] + mm(from_3[:, k:], out_2)
    turn = base + mm(first_s, outflow_2)
    outflow_1 = send(turn, (2, 1))
    from_3, out_2, _ = together(from_3, out_2, turn)
    in_3 = send(out_2, (2, 3))
    w_3 = from_3[:, k:]
    around = first_w + mm(first_s, mm(w_3, last_t))
    outflow_1, around = together(outflow_1, around)
    around = send(around, (2, 1))
    outflow_0 = send(base + mm(first_s, outflow_1), (1, 0))

    ahead, last_y, left_u = second_ahead(
        lower, upper, x, high, low, driver, probes,
        in_1, in_2, in_3, outflow_0, outflow_1, outflow_2,
    )

    in_1 = send(last_y, (0, 1))
    x, first_x = second_back(ahead, left_u)
    in_1, first_x, around = together(in_1, first_x, around)
    x_3 = send(first_x, (3, 2))
    base = first_x + mm(first_s, mm(w_3, last_y))
    x_3, base = together(x_3, base)
    joined = jnp.where(domain == 1, last_y + mm(last_t, in_1), base + mm(first_s, x_3))
    swapped = send(joined, (1, 2), (2, 1))
    past = mm(around, joined)
    base = jnp.where(
        domain == 1, first_x + mm(first_w, in_1) + mm(first_s, past), last_y
    )
    across = jnp.where(domain == 1, first_s, last_t)
    swapped, base, across, past = together(swapped, base, across, past)
    crossing = base + mm(across, swapped)
    ended = send(crossing, (1, 0), (2, 3))
    beyond = x_3 + mm(w_3, crossing)

    weight = weights / (k * energies)
    terms = charge(places, weight, energies, x, high, low, probes, in_1, swapped, swapped + past, beyond, ended)
    if energies == 8:
        half = energies // 2
        total = terms[:half] + near(terms[half:], (1,))[0]
        parts = [near(total[j], (2 * j,))[0] for j in range(1, half)]
        return total[0] + parts[0] + parts[1] + parts[2]
    split = terms.reshape(n, energies, b // energies).transpose(1, 0, 2)
    return jnp.sum(lax.all_to_all(split, "energy", 0, 0, tiled=True), axis=0)


def solution(mesh):
    placed = (
        P("energy", "dom", None, None),
        P("energy", "dom", None, None),
        P("energy", "dom", None, None),
        P("dom", "energy", None),
        P("dom"),
        P(),
        P("dom", None, None),
        P("energy"),
    )
    return jax.shard_map(
        per_device, mesh=mesh, in_specs=placed, out_specs=P("dom", "energy"), check_vma=False
    )
```

```python
import functools

import jax
import jax.numpy as jnp
from jax import lax
from jax.experimental import pallas as pl
from jax.experimental.pallas import tpu as pltpu
from jax.sharding import PartitionSpec as P

F32 = jnp.float32
BF16 = jnp.bfloat16
HIGH = lax.Precision.HIGH
MIB = 1 << 20


def halves(x):
    high = x.astype(BF16)
    return high, (x - high.astype(F32)).astype(BF16)


def dot(a, b):
    return jnp.dot(a, b, preferred_element_type=F32)


def left_two(a):
    return jnp.concatenate(halves(a), axis=1)


def left_three(a):
    high, low = halves(a)
    return jnp.concatenate([high, low, high], axis=1)


def apply_two(a, x):
    width = x.shape[1]
    both = jnp.concatenate(halves(x), axis=1)
    out = dot(a, jnp.concatenate([both, both], axis=0))
    return out[:, :width] + out[:, width:]


def apply_three(a, high, low):
    return dot(a, jnp.concatenate([high, high, low], axis=0))


def shapes(*entries):
    return [jax.ShapeDtypeStruct(shape, kind) for shape, kind in entries]


def cost(us):
    return pl.CostEstimate(flops=int(us * 1e9), bytes_accessed=0, transcendentals=0)


def params(mib):
    return pltpu.CompilerParams(vmem_limit_bytes=mib * MIB)


HBM = pl.BlockSpec(memory_space=pltpu.HBM)
VMEM = pl.BlockSpec(memory_space=pltpu.VMEM)
SMEM = pl.BlockSpec(memory_space=pltpu.SMEM)


def pinned(*entries):
    return [pltpu.VMEM(shape, kind) for shape, kind in entries]


def in_vmem(*arrays):
    return [pltpu.with_memory_space_constraint(x, pltpu.VMEM) for x in arrays]


def in_hbm(*arrays):
    return [pltpu.with_memory_space_constraint(x, pltpu.HBM) for x in arrays]


def local_kernel(
    pivot, lower, upper, probe,
    x_out, high_out, low_out, last_y, last_t, first_xw, first_x, first_w, first_s,
    d, l, u, z, left_a, left_b, given_a, given_b, h, x, high, low, sem, sem_out,
):
    n, b, k = z.shape
    kb = k + b
    wide = h.shape[2]
    lefts, givens = (left_a, left_b), (given_a, given_b)

    def load(which, i):
        src, dst = ((probe, z), (pivot, d), (lower, l), (upper, u))[which]
        return pltpu.make_async_copy(src.at[i], dst.at[i], sem.at[which, i])

    def store(which, i):
        src, dst = ((x, x_out), (high, high_out), (low, low_out))[which]
        return pltpu.make_async_copy(src.at[i], dst.at[i], sem_out.at[which, i])

    def begin(i, c):
        load(0, i).start()
        load(1, i).start()
        load(2, i).start()
        return c

    def begin_upper(i, c):
        load(3, n - 1 - i).start()
        return c

    lax.fori_loop(0, n, begin, 0)
    lax.fori_loop(0, n, begin_upper, 0)

    def arrive(i):
        load(0, i).wait()
        load(1, i).wait()
        load(2, i).wait()

    def prepare(i, slot):
        givens[slot][...] = apply_two(left_two(d[i]), z[i])
        lefts[slot][...] = left_three(l[i])

    def ahead(i, slot):
        moved = apply_three(lefts[slot][...], *halves(h[i - 1]))
        h[i, :, :k] = givens[slot][...] - moved[:, :k]
        h[i, :, k:] = -moved[:, k:]

    arrive(0)
    prepare(0, 0)
    h[0] = jnp.concatenate([given_a[...], -l[0], jnp.zeros((b, wide - kb), F32)], axis=1)
    arrive(1)
    prepare(1, 1)

    def ahead_pair(j, c):
        i = 2 * j + 1
        arrive(i + 1)
        ahead(i, 1)
        prepare(i + 1, 0)
        arrive(i + 2)
        ahead(i + 1, 0)
        prepare(i + 2, 1)
        return c

    lax.fori_loop(0, n // 2 - 1, ahead_pair, 0)

    def prepare_back(i, slot):
        lefts[slot][...] = left_three(u[i])

    def keep(i, value):
        value_high, value_low = halves(value)
        x[i] = value[:, :k]
        high[i] = value_high
        low[i] = value_low
        for which in range(3):
            store(which, i).start()

    def step_back(i, slot):
        moved = apply_three(lefts[slot][...], high[i + 1], low[i + 1])
        value = jnp.concatenate([h[i] - moved[:, :wide], -moved[:, wide:]], axis=1)
        keep(i, value)
        return value

    load(3, n - 1).wait()
    load(3, n - 2).wait()
    ahead(n - 1, 1)
    prepare_back(n - 1, 0)
    last_y[...] = h[n - 1, :, :k]
    last_t[...] = h[n - 1, :, k:kb]
    keep(n - 1, jnp.concatenate([h[n - 1, :, :kb], -u[n - 1]], axis=1))
    prepare_back(n - 2, 0)

    def back_pair(j, c):
        i = n - 2 - 2 * j
        load(3, i - 1).wait()
        step_back(i, 0)
        prepare_back(i - 1, 1)
        load(3, i - 2).wait()
        step_back(i - 1, 1)
        prepare_back(i - 2, 0)
        return c

    lax.fori_loop(0, n // 2 - 1, back_pair, 0)
    value = step_back(0, 0)
    first_xw[...] = value[:, :kb]
    first_x[...] = value[:, :k]
    first_w[...] = value[:, k:kb]
    first_s[...] = value[:, kb:]

    def drain(i, c):
        for which in range(3):
            store(which, i).wait()
        return c

    lax.fori_loop(0, n, drain, 0)


def local_maps(pivots, lower, upper, probes):
    n, b, k = probes.shape
    wide = -(-(k + b) // 128) * 128
    full = k + 2 * b
    v = pltpu.VMEM
    return pl.pallas_call(
        local_kernel,
        in_specs=[HBM] * 4,
        out_specs=[HBM] * 3 + [VMEM] * 6,
        out_shape=[
            pltpu.HBM((n, b, k), F32),
            pltpu.HBM((n, b, full), BF16),
            pltpu.HBM((n, b, full), BF16),
        ]
        + pinned(
            ((b, k), F32),
            ((b, b), F32),
            ((b, k + b), F32),
            ((b, k), F32),
            ((b, b), F32),
            ((b, b), F32),
        ),
        scratch_shapes=[
            v((n, b, b), F32),
            v((n, b, b), F32),
            v((n, b, b), F32),
            v((n, b, k), F32),
            v((b, 3 * b), BF16),
            v((b, 3 * b), BF16),
            v((b, k), F32),
            v((b, k), F32),
            v((n, b, wide), F32),
            v((n, b, k), F32),
            v((n, b, full), BF16),
            v((n, b, full), BF16),
            pltpu.SemaphoreType.DMA((4, n)),
            pltpu.SemaphoreType.DMA((3, n)),
        ],
        compiler_params=params(52),
        cost_estimate=cost(15),
        name="local_maps",
    )(*in_hbm(pivots, lower, upper, probes))


def drive_kernel(start, me, scale, pivot, *rest):
    pieces, out, gathered = rest[:-2], rest[-2], rest[-1]
    step = pl.program_id(0)
    if len(pieces) > 1:
        rows = pieces[0].shape[1]
        for j, piece in enumerate(pieces):
            owner = lax.bitwise_xor(me[0], j)
            gathered[pl.ds(pl.multiple_of(owner * rows, 8), rows), :] = piece[0]
        potential = gathered[...]
    else:
        potential = pieces[0][0]
    out[step] = left_two(apply_three(left_three(pivot[0]), *halves(potential * scale[step + start])))


def drive(start, stop, me, scale, pivots, pieces):
    b = pivots.shape[1]
    rows = pieces[0].shape[1]
    at = lambda i: (i + start, 0, 0)
    return pl.pallas_call(
        functools.partial(drive_kernel, start),
        grid=(stop - start,),
        in_specs=[SMEM, SMEM, pl.BlockSpec((1, b, b), at)]
        + [pl.BlockSpec((1, rows, b), at)] * len(pieces),
        out_specs=VMEM,
        out_shape=pltpu.VMEM((stop - start, b, 2 * b), BF16),
        scratch_shapes=[pltpu.VMEM((b, b), F32)],
        compiler_params=params(10),
        cost_estimate=cost(0.01),
        name="drive_maps",
    )(me, scale, *in_hbm(pivots, *pieces))


def add_flows(x, high, low, i, flows):
    n, b, k = x.shape
    skip = high.shape[2] - flows.shape[0]
    rows = lambda ref: ref[pl.ds(i, 2), :, skip:].reshape(2 * b, flows.shape[0])
    out = dot(rows(high), flows) + dot(rows(low), flows)
    out = out[:, :k] + out[:, k:]
    return x[i] + out[:b], x[i + 1] + out[b:]


def sweep_ahead(
    lower, upper, x, high, low, drive_a, drive_b, inflow, outflow, y, u, l, left_a, left_b, sem
):
    n, b, k = x.shape
    lefts = (left_a, left_b)
    load_l = lambda i: pltpu.make_async_copy(lower.at[i], l.at[i], sem.at[0, i])
    load_u = lambda i: pltpu.make_async_copy(upper.at[i], u.at[i], sem.at[1, i])

    def begin(i, c):
        load_l(i).start()
        load_u(i).start()
        return c

    lax.fori_loop(0, n, begin, 0)
    flows = jnp.concatenate(halves(jnp.concatenate([inflow, outflow], axis=0)), axis=1)
    half = drive_a.shape[0]
    for start, driver in ((0, drive_a), (half, drive_b)):

        def given(r, c):
            j = 2 * r
            i = j + start
            ahead_0, ahead_1 = add_flows(x, high, low, i, flows)
            y[i] = apply_two(driver[j], ahead_0)
            y[i + 1] = apply_two(driver[j + 1], ahead_1)
            return c

        lax.fori_loop(0, driver.shape[0] // 2, given, 0)

    def arrive(i, c):
        load_l(i).wait()
        load_u(i).wait()
        return c

    lax.fori_loop(0, n, arrive, 0)
    left_b[...] = left_two(l[1])

    def step(i, slot):
        y[i] = y[i] - apply_two(lefts[slot][...], y[i - 1])

    def pair(j, c):
        i = 2 * j + 1
        step(i, 1)
        left_a[...] = left_two(l[i + 1])
        step(i + 1, 0)
        left_b[...] = left_two(l[i + 2])
        return c

    lax.fori_loop(0, n // 2 - 1, pair, 0)
    step(n - 1, 1)


def sweep_back(y, u, x_out, out, left_a, left_b, sem):
    n = y.shape[0]
    lefts = (left_a, left_b)
    store = lambda i: pltpu.make_async_copy(out.at[i], x_out.at[i], sem.at[i])
    left_a[...] = left_two(u[n - 2])
    out[n - 1] = y[n - 1]
    store(n - 1).start()

    def step(i, slot):
        out[i] = y[i] - apply_two(lefts[slot][...], out[i + 1])
        store(i).start()

    def pair(j, c):
        i = n - 2 - 2 * j
        step(i, 0)
        left_b[...] = left_two(u[i - 1])
        step(i - 1, 1)
        left_a[...] = left_two(u[i - 2])
        return c

    lax.fori_loop(0, n // 2 - 1, pair, 0)
    step(0, 0)

    def drain(i, c):
        store(i).wait()
        return c

    lax.fori_loop(0, n, drain, 0)


def second_of_3_kernel(
    places, lower, upper, x, high, low, drive_a, drive_b, probes, in_3,
    x_out, first, y, u, out, l, left_a, left_b, sem, sem_out,
):
    @pl.when(places[0] == 3)
    def _():
        inflow = in_3[...]
        sweep_ahead(
            lower, upper, x, high, low, drive_a, drive_b, inflow, jnp.zeros_like(inflow),
            y, u, l, left_a, left_b, sem,
        )
        sweep_back(y, u, x_out, out, left_a, left_b, sem_out)
        first[...] = out[0]

    @pl.when(places[0] != 3)
    def _():
        first[...] = jnp.zeros_like(first)


def second_of_3(places, lower, upper, x, high, low, drive_a, drive_b, probes, in_3):
    n, b, k = x.shape
    v = pltpu.VMEM
    return pl.pallas_call(
        second_of_3_kernel,
        in_specs=[SMEM] + [HBM] * 2 + [VMEM] * 7,
        out_specs=[HBM, VMEM],
        out_shape=[pltpu.HBM((n, b, k), F32), pltpu.VMEM((b, k), F32)],
        scratch_shapes=[
            v((n, b, k), F32),
            v((n, b, b), F32),
            v((n, b, k), F32),
            v((n, b, b), F32),
            v((b, 2 * b), BF16),
            v((b, 2 * b), BF16),
            pltpu.SemaphoreType.DMA((2, n)),
            pltpu.SemaphoreType.DMA((n,)),
        ],
        compiler_params=params(18),
        cost_estimate=cost(0.01),
        name="second_of_3",
    )(places, *in_hbm(lower, upper), *in_vmem(x, high, low, drive_a, drive_b, probes), in_3)


def second_ahead_kernel(
    places, lower, upper, x, high, low, drive_a, drive_b, in_1, in_2, out_0, out_1, out_2,
    y, u, last, l, left_a, left_b, sem,
):
    @pl.when(places[0] != 3)
    def _():
        inflow = in_1[...] + in_2[...]
        outflow = out_0[...] + out_1[...] + out_2[...]
        sweep_ahead(
            lower, upper, x, high, low, drive_a, drive_b, inflow, outflow,
            y, u, l, left_a, left_b, sem,
        )
        last[...] = y[y.shape[0] - 1]

    @pl.when(places[0] == 3)
    def _():
        last[...] = jnp.zeros_like(last)


def second_ahead(places, lower, upper, x, high, low, drive_a, drive_b, *flows):
    n, b, k = x.shape
    return pl.pallas_call(
        second_ahead_kernel,
        in_specs=[SMEM] + [HBM] * 2 + [VMEM] * (5 + len(flows)),
        out_specs=[VMEM] * 3,
        out_shape=pinned(((n, b, k), F32), ((n, b, b), F32), ((b, k), F32)),
        scratch_shapes=[
            pltpu.VMEM((n, b, b), F32),
            pltpu.VMEM((b, 2 * b), BF16),
            pltpu.VMEM((b, 2 * b), BF16),
            pltpu.SemaphoreType.DMA((2, n)),
        ],
        compiler_params=params(12),
        cost_estimate=cost(0.01),
        name="second_ahead",
    )(places, *in_hbm(lower, upper), *in_vmem(x, high, low, drive_a, drive_b), *flows)


def second_back_kernel(places, y, u, x_of_3, x_out, first, out, left_a, left_b, sem):
    @pl.when(places[0] != 3)
    def _():
        sweep_back(y, u, x_out, out, left_a, left_b, sem)
        first[...] = out[0]

    @pl.when(places[0] == 3)
    def _():
        first[...] = jnp.zeros_like(first)


def second_back(places, y, u, x_of_3):
    n, b, k = y.shape
    return pl.pallas_call(
        second_back_kernel,
        in_specs=[SMEM] + [VMEM] * 2 + [HBM],
        out_specs=[HBM, VMEM],
        out_shape=[pltpu.HBM((n, b, k), F32), pltpu.VMEM((b, k), F32)],
        input_output_aliases={3: 0},
        scratch_shapes=[
            pltpu.VMEM((n, b, k), F32),
            pltpu.VMEM((b, 2 * b), BF16),
            pltpu.VMEM((b, 2 * b), BF16),
            pltpu.SemaphoreType.DMA((n,)),
        ],
        compiler_params=params(5),
        cost_estimate=cost(0.01),
        name="second_back",
    )(places, *in_vmem(y, u), *in_hbm(x_of_3))


def charge_kernel(places, weight, x, high, low, probe, in_1, in_2, out_1, out_2, ended, *outs):
    n, b, k = x.shape
    at, energy = places[0], places[1]
    none = jnp.zeros_like(ended)
    inflow = jnp.where(at == 1, in_1[...], jnp.where(at == 2, in_2[...], none))
    inflow = jnp.where(at == 3, ended[...], inflow)
    outflow = jnp.where(at == 1, out_1[...], jnp.where(at == 2, out_2[...], none))
    outflow = jnp.where(at == 0, ended[...], outflow)
    flows = jnp.concatenate(halves(jnp.concatenate([inflow, outflow], axis=0)), axis=1)
    terms = outs[-1]
    for i in range(0, n, 2):
        for j, value in enumerate(add_flows(x, high, low, i, flows)):
            charges = jnp.sum((value * probe[i + j]).T, axis=0, keepdims=True)
            terms[i + j : i + j + 1, :] = charges * weight[0]
    if len(outs) > 1:
        blocks = outs[0]
        owners, _, rows = blocks.shape
        for owner in range(owners):
            j = lax.bitwise_xor(energy, owner)
            blocks[lax.div(j, 2) + lax.rem(j, 2) * (owners // 2)] = terms[:, owner * rows : (owner + 1) * rows]


def charge(places, weight, energies, x, high, low, probes, *flows):
    n, b, k = probes.shape
    by_swaps = energies == 8
    return pl.pallas_call(
        charge_kernel,
        in_specs=[SMEM] * 2 + [VMEM] * (4 + len(flows)),
        out_specs=VMEM,
        out_shape=pltpu.VMEM((energies, n, b // energies) if by_swaps else (n, b), F32),
        scratch_shapes=[pltpu.VMEM((n, b), F32)] if by_swaps else [],
        compiler_params=params(10),
        name="charge_terms",
    )(places, weight, *in_vmem(x, high, low, probes), *flows)


def mm(a, b):
    return jnp.dot(a, b, precision=HIGH)


def send(x, *pairs):
    return lax.ppermute(x, "dom", list(pairs))


def near(x, ways):
    peers = lax.axis_size("energy")
    return [lax.ppermute(x, "energy", [(i, i ^ way) for i in range(peers)]) for way in ways]


def together(*values):
    return lax.optimization_barrier(values)


def per_device(
    pivots, lower_spikes, upper_spikes, potential, grain_of_slice, grain_shift, probes, weights
):
    pivots, lower, upper = pivots[0], lower_spikes[0], upper_spikes[0]
    k = probes.shape[2]
    energies = lax.axis_size("energy")
    me = lax.axis_index("energy").astype(jnp.int32).reshape(1)
    domain = lax.axis_index("dom")
    grain_count = grain_shift.shape[0]
    grain_match = grain_of_slice[:, None] == jnp.arange(grain_count, dtype=jnp.int32)[None, :]
    grain_scale = jnp.sum(jnp.where(grain_match, grain_shift[None, :], 0.0), axis=1)
    by_swaps = energies == 8 and potential.shape[1] % 8 == 0

    places = jnp.stack([domain, lax.axis_index("energy")]).astype(jnp.int32)
    n, b = pivots.shape[:2]

    even = near(potential, (2, 4, 6)) if by_swaps else []
    x, high, low, last_y, last_t, first_xw, first_x, first_w, first_s = local_maps(
        pivots, lower, upper, probes
    )

    if by_swaps:
        last_y, even[0] = together(last_y, even[0])
    in_1 = send(last_y, (0, 1))
    from_3 = send(first_xw, (3, 2))
    if by_swaps:
        in_1, even[1], even[2] = together(in_1, even[1], even[2])
    out_1 = last_y + mm(last_t, in_1)
    in_2 = send(out_1, (1, 2))
    if by_swaps:
        even = [potential] + even
        odd = [near(block, (1,))[0] for block in even]
        pieces = [block for pair in zip(even, odd) for block in pair]
    else:
        pieces = [lax.all_gather(potential, "energy", axis=1, tiled=True)]
    drive_a = drive(0, n // 2, me, grain_scale, pivots, pieces)
    in_2, from_3, drive_a = together(in_2, from_3, drive_a)
    out_2 = last_y + mm(last_t, in_2)
    base = first_x + mm(first_w, in_1 + in_2)
    outflow_2 = from_3[:, :k] + mm(from_3[:, k:], out_2)
    turn = base + mm(first_s, outflow_2)
    outflow_1 = send(turn, (2, 1))
    from_3, out_2, scale, _ = together(from_3, out_2, grain_scale, turn)
    in_3 = send(out_2, (2, 3))
    drive_b = drive(n // 2, n, me, scale, pivots, pieces)
    w_3 = from_3[:, k:]
    around = first_w + mm(first_s, mm(w_3, last_t))
    outflow_1, drive_b, around = together(outflow_1, drive_b, around)
    around = send(around, (2, 1))
    outflow_0 = send(base + mm(first_s, outflow_1), (1, 0))

    x_of_3, first_of_3 = second_of_3(
        places, lower, upper, x, high, low, drive_a, drive_b, probes, in_3
    )
    x_3 = send(first_of_3, (3, 2))
    outflow_0, x_of_3 = together(outflow_0, x_of_3)
    ahead, u, last_y = second_ahead(
        places, lower, upper, x, high, low, drive_a, drive_b,
        in_1, in_2, outflow_0, outflow_1, outflow_2,
    )

    in_1 = send(last_y, (0, 1))
    x, first_x = second_back(places, ahead, u, x_of_3)
    in_1, first_x, around = together(in_1, first_x, around)
    base = first_x + mm(first_s, mm(w_3, last_y))
    x_3, base = together(x_3, base)
    joined = jnp.where(domain == 1, last_y + mm(last_t, in_1), base + mm(first_s, x_3))
    swapped = send(joined, (1, 2), (2, 1))
    past = mm(around, joined)
    base = jnp.where(
        domain == 1, first_x + mm(first_w, in_1) + mm(first_s, past), last_y
    )
    across = jnp.where(domain == 1, first_s, last_t)
    swapped, base, across, past = together(swapped, base, across, past)
    crossing = base + mm(across, swapped)
    ended = send(crossing, (1, 0), (2, 3))
    beyond = x_3 + mm(w_3, crossing)

    weight = weights / (k * energies)
    terms = charge(places, weight, energies, x, high, low, probes, in_1, swapped, swapped + past, beyond, ended)
    if energies == 8:
        half = energies // 2
        total = terms[:half] + near(terms[half:], (1,))[0]
        parts = [near(total[j], (2 * j,))[0] for j in range(1, half)]
        return total[0] + parts[0] + parts[1] + parts[2]
    split = terms.reshape(n, energies, b // energies).transpose(1, 0, 2)
    return jnp.sum(lax.all_to_all(split, "energy", 0, 0, tiled=True), axis=0)


def solution(mesh):
    placed = (
        P("energy", "dom", None, None),
        P("energy", "dom", None, None),
        P("energy", "dom", None, None),
        P("dom", "energy", None),
        P("dom"),
        P(),
        P("dom", None, None),
        P("energy"),
    )
    return jax.shard_map(
        per_device, mesh=mesh, in_specs=placed, out_specs=P("dom", "energy"), check_vma=False
    )
```

```python
import functools

import jax
import jax.numpy as jnp
from jax import lax
from jax.experimental import pallas as pl
from jax.experimental.pallas import tpu as pltpu
from jax.sharding import PartitionSpec as P

F32 = jnp.float32
BF16 = jnp.bfloat16
HIGH = lax.Precision.HIGH
MIB = 1 << 20


def halves(x):
    high = x.astype(BF16)
    return high, (x - high.astype(F32)).astype(BF16)


def dot(a, b):
    return jnp.dot(a, b, preferred_element_type=F32)


def left_two(a):
    return jnp.concatenate(halves(a), axis=1)


def left_three(a):
    high, low = halves(a)
    return jnp.concatenate([high, low, high], axis=1)


def apply_two(a, x):
    width = x.shape[1]
    both = jnp.concatenate(halves(x), axis=1)
    out = dot(a, jnp.concatenate([both, both], axis=0))
    return out[:, :width] + out[:, width:]


def apply_three(a, high, low):
    return dot(a, jnp.concatenate([high, high, low], axis=0))


def shapes(*entries):
    return [jax.ShapeDtypeStruct(shape, kind) for shape, kind in entries]


def cost(us):
    return pl.CostEstimate(flops=int(us * 1e9), bytes_accessed=0, transcendentals=0)


def params(mib):
    return pltpu.CompilerParams(vmem_limit_bytes=mib * MIB)


HBM = pl.BlockSpec(memory_space=pltpu.HBM)
VMEM = pl.BlockSpec(memory_space=pltpu.VMEM)
SMEM = pl.BlockSpec(memory_space=pltpu.SMEM)


def pinned(*entries):
    return [pltpu.VMEM(shape, kind) for shape, kind in entries]


def in_vmem(*arrays):
    return [pltpu.with_memory_space_constraint(x, pltpu.VMEM) for x in arrays]


def in_hbm(*arrays):
    return [pltpu.with_memory_space_constraint(x, pltpu.HBM) for x in arrays]


def local_kernel(
    pivot, lower, upper, probe,
    x_out, high_out, low_out, last_y, last_t, first_xw, first_x, first_w, first_s,
    d, l, u, z, left_a, left_b, given_a, given_b, h, x, high, low, sem, sem_out,
):
    n, b, k = z.shape
    kb = k + b
    wide = h.shape[2]
    lefts, givens = (left_a, left_b), (given_a, given_b)

    def load(which, i):
        src, dst = ((probe, z), (pivot, d), (lower, l), (upper, u))[which]
        return pltpu.make_async_copy(src.at[i], dst.at[i], sem.at[which, i])

    def store(which, i):
        src, dst = ((x, x_out), (high, high_out), (low, low_out))[which]
        return pltpu.make_async_copy(src.at[i], dst.at[i], sem_out.at[which, i])

    def begin(i, c):
        load(0, i).start()
        load(1, i).start()
        load(2, i).start()
        return c

    def begin_upper(i, c):
        load(3, n - 1 - i).start()
        return c

    lax.fori_loop(0, n, begin, 0)
    lax.fori_loop(0, n, begin_upper, 0)

    def arrive(i):
        load(0, i).wait()
        load(1, i).wait()
        load(2, i).wait()

    def prepare(i, slot):
        givens[slot][...] = apply_two(left_two(d[i]), z[i])
        lefts[slot][...] = left_three(l[i])

    def ahead(i, slot):
        moved = apply_three(lefts[slot][...], *halves(h[i - 1]))
        h[i, :, :k] = givens[slot][...] - moved[:, :k]
        h[i, :, k:] = -moved[:, k:]

    arrive(0)
    prepare(0, 0)
    h[0] = jnp.concatenate([given_a[...], -l[0], jnp.zeros((b, wide - kb), F32)], axis=1)
    arrive(1)
    prepare(1, 1)

    def ahead_pair(j, c):
        i = 2 * j + 1
        arrive(i + 1)
        ahead(i, 1)
        prepare(i + 1, 0)
        arrive(i + 2)
        ahead(i + 1, 0)
        prepare(i + 2, 1)
        return c

    lax.fori_loop(0, n // 2 - 1, ahead_pair, 0)

    def prepare_back(i, slot):
        lefts[slot][...] = left_three(u[i])

    def keep(i, value):
        value_high, value_low = halves(value)
        x[i] = value[:, :k]
        high[i] = value_high
        low[i] = value_low
        for which in range(3):
            store(which, i).start()

    def step_back(i, slot):
        moved = apply_three(lefts[slot][...], high[i + 1], low[i + 1])
        value = jnp.concatenate([h[i] - moved[:, :wide], -moved[:, wide:]], axis=1)
        keep(i, value)
        return value

    load(3, n - 1).wait()
    load(3, n - 2).wait()
    ahead(n - 1, 1)
    prepare_back(n - 1, 0)
    last_y[...] = h[n - 1, :, :k]
    last_t[...] = h[n - 1, :, k:kb]
    keep(n - 1, jnp.concatenate([h[n - 1, :, :kb], -u[n - 1]], axis=1))
    prepare_back(n - 2, 0)

    def back_pair(j, c):
        i = n - 2 - 2 * j
        load(3, i - 1).wait()
        step_back(i, 0)
        prepare_back(i - 1, 1)
        load(3, i - 2).wait()
        step_back(i - 1, 1)
        prepare_back(i - 2, 0)
        return c

    lax.fori_loop(0, n // 2 - 1, back_pair, 0)
    value = step_back(0, 0)
    first_xw[...] = value[:, :kb]
    first_x[...] = value[:, :k]
    first_w[...] = value[:, k:kb]
    first_s[...] = value[:, kb:]

    def drain(i, c):
        for which in range(3):
            store(which, i).wait()
        return c

    lax.fori_loop(0, n, drain, 0)


def local_maps(pivots, lower, upper, probes):
    n, b, k = probes.shape
    wide = -(-(k + b) // 128) * 128
    full = k + 2 * b
    v = pltpu.VMEM
    return pl.pallas_call(
        local_kernel,
        in_specs=[HBM] * 4,
        out_specs=[HBM] * 3 + [VMEM] * 6,
        out_shape=[
            pltpu.HBM((n, b, k), F32),
            pltpu.HBM((n, b, full), BF16),
            pltpu.HBM((n, b, full), BF16),
        ]
        + pinned(
            ((b, k), F32),
            ((b, b), F32),
            ((b, k + b), F32),
            ((b, k), F32),
            ((b, b), F32),
            ((b, b), F32),
        ),
        scratch_shapes=[
            v((n, b, b), F32),
            v((n, b, b), F32),
            v((n, b, b), F32),
            v((n, b, k), F32),
            v((b, 3 * b), BF16),
            v((b, 3 * b), BF16),
            v((b, k), F32),
            v((b, k), F32),
            v((n, b, wide), F32),
            v((n, b, k), F32),
            v((n, b, full), BF16),
            v((n, b, full), BF16),
            pltpu.SemaphoreType.DMA((4, n)),
            pltpu.SemaphoreType.DMA((3, n)),
        ],
        compiler_params=params(52),
        cost_estimate=cost(15),
        name="local_maps",
    )(*in_hbm(pivots, lower, upper, probes))


def drive_kernel(start, me, scale, pivot, *rest):
    pieces, out, gathered = rest[:-2], rest[-2], rest[-1]
    step = pl.program_id(0)
    for i in range(2):
        if len(pieces) > 1:
            rows = pieces[0].shape[1]
            for j, piece in enumerate(pieces):
                owner = lax.bitwise_xor(me[0], j)
                gathered[i, pl.ds(pl.multiple_of(owner * rows, 8), rows), :] = piece[i]
            potential = gathered[i]
        else:
            potential = pieces[0][i]
        potential = potential * scale[2 * step + i + start]
        out[2 * step + i] = left_two(apply_three(left_three(pivot[i]), *halves(potential)))


def drive(start, stop, me, scale, pivots, pieces):
    b = pivots.shape[1]
    rows = pieces[0].shape[1]
    at = lambda i: (i + start // 2, 0, 0)
    return pl.pallas_call(
        functools.partial(drive_kernel, start),
        grid=((stop - start) // 2,),
        in_specs=[SMEM, SMEM, pl.BlockSpec((2, b, b), at)]
        + [pl.BlockSpec((2, rows, b), at)] * len(pieces),
        out_specs=VMEM,
        out_shape=pltpu.VMEM((stop - start, b, 2 * b), BF16),
        scratch_shapes=[pltpu.VMEM((2, b, b), F32)],
        compiler_params=params(14),
        cost_estimate=cost(0.01),
        name="drive_maps",
    )(me, scale, *in_hbm(pivots, *pieces))


def add_flows(x, high, low, i, flows):
    n, b, k = x.shape
    skip = high.shape[2] - flows.shape[0]
    rows = lambda ref: ref[pl.ds(i, 2), :, skip:].reshape(2 * b, flows.shape[0])
    out = dot(rows(high), flows) + dot(rows(low), flows)
    out = out[:, :k] + out[:, k:]
    return x[i] + out[:b], x[i + 1] + out[b:]


def sweep_ahead(
    lower, upper, x, high, low, drive_a, drive_b, inflow, outflow, y, u, l, left_a, left_b, sem
):
    n, b, k = x.shape
    lefts = (left_a, left_b)
    load_l = lambda i: pltpu.make_async_copy(lower.at[i], l.at[i], sem.at[0, i])
    load_u = lambda i: pltpu.make_async_copy(upper.at[i], u.at[i], sem.at[1, i])

    def begin(i, c):
        load_l(i).start()
        load_u(i).start()
        return c

    lax.fori_loop(0, n, begin, 0)
    flows = jnp.concatenate(halves(jnp.concatenate([inflow, outflow], axis=0)), axis=1)
    half = drive_a.shape[0]
    for start, driver in ((0, drive_a), (half, drive_b)):

        def given(r, c):
            j = 2 * r
            i = j + start
            ahead_0, ahead_1 = add_flows(x, high, low, i, flows)
            y[i] = apply_two(driver[j], ahead_0)
            y[i + 1] = apply_two(driver[j + 1], ahead_1)
            return c

        lax.fori_loop(0, driver.shape[0] // 2, given, 0)

    def arrive(i, c):
        load_l(i).wait()
        load_u(i).wait()
        return c

    lax.fori_loop(0, n, arrive, 0)
    left_b[...] = left_two(l[1])

    def step(i, slot):
        y[i] = y[i] - apply_two(lefts[slot][...], y[i - 1])

    def pair(j, c):
        i = 2 * j + 1
        step(i, 1)
        left_a[...] = left_two(l[i + 1])
        step(i + 1, 0)
        left_b[...] = left_two(l[i + 2])
        return c

    lax.fori_loop(0, n // 2 - 1, pair, 0)
    step(n - 1, 1)


def sweep_back(y, u, x_out, out, left_a, left_b, sem):
    n = y.shape[0]
    lefts = (left_a, left_b)
    store = lambda i: pltpu.make_async_copy(out.at[i], x_out.at[i], sem.at[i])
    left_a[...] = left_two(u[n - 2])
    out[n - 1] = y[n - 1]
    store(n - 1).start()

    def step(i, slot):
        out[i] = y[i] - apply_two(lefts[slot][...], out[i + 1])
        store(i).start()

    def pair(j, c):
        i = n - 2 - 2 * j
        step(i, 0)
        left_b[...] = left_two(u[i - 1])
        step(i - 1, 1)
        left_a[...] = left_two(u[i - 2])
        return c

    lax.fori_loop(0, n // 2 - 1, pair, 0)
    step(0, 0)

    def drain(i, c):
        store(i).wait()
        return c

    lax.fori_loop(0, n, drain, 0)


def second_of_3_kernel(
    places, lower, upper, x, high, low, drive_a, drive_b, probes, in_3,
    x_out, first, y, u, out, l, left_a, left_b, sem, sem_out,
):
    @pl.when(places[0] == 3)
    def _():
        inflow = in_3[...]
        sweep_ahead(
            lower, upper, x, high, low, drive_a, drive_b, inflow, jnp.zeros_like(inflow),
            y, u, l, left_a, left_b, sem,
        )
        sweep_back(y, u, x_out, out, left_a, left_b, sem_out)
        first[...] = out[0]

    @pl.when(places[0] != 3)
    def _():
        first[...] = jnp.zeros_like(first)


def second_of_3(places, lower, upper, x, high, low, drive_a, drive_b, probes, in_3):
    n, b, k = x.shape
    v = pltpu.VMEM
    return pl.pallas_call(
        second_of_3_kernel,
        in_specs=[SMEM] + [HBM] * 2 + [VMEM] * 7,
        out_specs=[HBM, VMEM],
        out_shape=[pltpu.HBM((n, b, k), F32), pltpu.VMEM((b, k), F32)],
        scratch_shapes=[
            v((n, b, k), F32),
            v((n, b, b), F32),
            v((n, b, k), F32),
            v((n, b, b), F32),
            v((b, 2 * b), BF16),
            v((b, 2 * b), BF16),
            pltpu.SemaphoreType.DMA((2, n)),
            pltpu.SemaphoreType.DMA((n,)),
        ],
        compiler_params=params(18),
        cost_estimate=cost(0.01),
        name="second_of_3",
    )(places, *in_hbm(lower, upper), *in_vmem(x, high, low, drive_a, drive_b, probes), in_3)


def second_ahead_kernel(
    places, lower, upper, x, high, low, drive_a, drive_b, in_1, in_2, out_0, out_1, out_2,
    y, u, last, l, left_a, left_b, sem,
):
    @pl.when(places[0] != 3)
    def _():
        inflow = in_1[...] + in_2[...]
        outflow = out_0[...] + out_1[...] + out_2[...]
        sweep_ahead(
            lower, upper, x, high, low, drive_a, drive_b, inflow, outflow,
            y, u, l, left_a, left_b, sem,
        )
        last[...] = y[y.shape[0] - 1]

    @pl.when(places[0] == 3)
    def _():
        last[...] = jnp.zeros_like(last)


def second_ahead(places, lower, upper, x, high, low, drive_a, drive_b, *flows):
    n, b, k = x.shape
    return pl.pallas_call(
        second_ahead_kernel,
        in_specs=[SMEM] + [HBM] * 2 + [VMEM] * (5 + len(flows)),
        out_specs=[VMEM] * 3,
        out_shape=pinned(((n, b, k), F32), ((n, b, b), F32), ((b, k), F32)),
        scratch_shapes=[
            pltpu.VMEM((n, b, b), F32),
            pltpu.VMEM((b, 2 * b), BF16),
            pltpu.VMEM((b, 2 * b), BF16),
            pltpu.SemaphoreType.DMA((2, n)),
        ],
        compiler_params=params(12),
        cost_estimate=cost(0.01),
        name="second_ahead",
    )(places, *in_hbm(lower, upper), *in_vmem(x, high, low, drive_a, drive_b), *flows)


def second_back_kernel(places, y, u, x_of_3, x_out, first, out, left_a, left_b, sem):
    @pl.when(places[0] != 3)
    def _():
        sweep_back(y, u, x_out, out, left_a, left_b, sem)
        first[...] = out[0]

    @pl.when(places[0] == 3)
    def _():
        first[...] = jnp.zeros_like(first)


def second_back(places, y, u, x_of_3):
    n, b, k = y.shape
    return pl.pallas_call(
        second_back_kernel,
        in_specs=[SMEM] + [VMEM] * 2 + [HBM],
        out_specs=[HBM, VMEM],
        out_shape=[pltpu.HBM((n, b, k), F32), pltpu.VMEM((b, k), F32)],
        input_output_aliases={3: 0},
        scratch_shapes=[
            pltpu.VMEM((n, b, k), F32),
            pltpu.VMEM((b, 2 * b), BF16),
            pltpu.VMEM((b, 2 * b), BF16),
            pltpu.SemaphoreType.DMA((n,)),
        ],
        compiler_params=params(5),
        cost_estimate=cost(0.01),
        name="second_back",
    )(places, *in_vmem(y, u), *in_hbm(x_of_3))


def charge_kernel(places, weight, x, high, low, probe, in_1, in_2, out_1, out_2, ended, blocks, terms):
    n, b, k = x.shape
    at = places[0]
    none = jnp.zeros_like(ended)
    inflow = jnp.where(at == 1, in_1[...], jnp.where(at == 2, in_2[...], none))
    inflow = jnp.where(at == 3, ended[...], inflow)
    outflow = jnp.where(at == 1, out_1[...], jnp.where(at == 2, out_2[...], none))
    outflow = jnp.where(at == 0, ended[...], outflow)
    flows = jnp.concatenate(halves(jnp.concatenate([inflow, outflow], axis=0)), axis=1)
    skip = high.shape[2] - flows.shape[0]
    for i in range(n):
        maps = jnp.concatenate([high[i, :, skip:], low[i, :, skip:]], axis=1)
        out = dot(maps, jnp.concatenate([flows, flows], axis=0))
        value = x[i] + out[:, :k] + out[:, k:]
        terms[i : i + 1, :] = jnp.sum((value * probe[i]).T, axis=0, keepdims=True) * weight[0]
    owners = blocks.shape[0]
    rows = b // owners
    for owner in range(owners):
        blocks[owner, :, :rows] = terms[:, owner * rows : (owner + 1) * rows]


def charge(places, weight, energies, x, high, low, probes, *flows):
    n, b, k = probes.shape
    wide = -(-(b // energies) // 128) * 128
    return pl.pallas_call(
        charge_kernel,
        in_specs=[SMEM] * 2 + [VMEM] * (4 + len(flows)),
        out_specs=VMEM,
        out_shape=pltpu.VMEM((energies, n, wide), F32),
        scratch_shapes=[pltpu.VMEM((n, b), F32)],
        compiler_params=params(10),
        name="charge_terms",
    )(places, weight, *in_vmem(x, high, low, probes), *flows)


def mm(a, b):
    return jnp.dot(a, b, precision=HIGH)


def send(x, *pairs):
    return lax.ppermute(x, "dom", list(pairs))


def near(x, ways):
    peers = lax.axis_size("energy")
    return [lax.ppermute(x, "energy", [(i, i ^ way) for i in range(peers)]) for way in ways]


def together(*values):
    return lax.optimization_barrier(values)


def per_device(
    pivots, lower_spikes, upper_spikes, potential, grain_of_slice, grain_shift, probes, weights
):
    pivots, lower, upper = pivots[0], lower_spikes[0], upper_spikes[0]
    k = probes.shape[2]
    energies = lax.axis_size("energy")
    me = lax.axis_index("energy").astype(jnp.int32).reshape(1)
    domain = lax.axis_index("dom")
    grain_count = grain_shift.shape[0]
    grain_match = grain_of_slice[:, None] == jnp.arange(grain_count, dtype=jnp.int32)[None, :]
    grain_scale = jnp.sum(jnp.where(grain_match, grain_shift[None, :], 0.0), axis=1)
    by_swaps = energies == 8 and potential.shape[1] % 8 == 0

    places = jnp.stack([domain, lax.axis_index("energy")]).astype(jnp.int32)
    n, b = pivots.shape[:2]

    even = near(potential, (2, 4, 6)) if by_swaps else []
    x, high, low, last_y, last_t, first_xw, first_x, first_w, first_s = local_maps(
        pivots, lower, upper, probes
    )

    if by_swaps:
        last_y, even[0] = together(last_y, even[0])
    in_1 = send(last_y, (0, 1))
    from_3 = send(first_xw, (3, 2))
    if by_swaps:
        in_1, even[1], even[2] = together(in_1, even[1], even[2])
    out_1 = last_y + mm(last_t, in_1)
    in_2 = send(out_1, (1, 2))
    if by_swaps:
        even = [potential] + even
        odd = [near(block, (1,))[0] for block in even]
        pieces = [block for pair in zip(even, odd) for block in pair]
    else:
        pieces = [lax.all_gather(potential, "energy", axis=1, tiled=True)]
    drive_a = drive(0, n // 2, me, grain_scale, pivots, pieces)
    in_2, from_3, drive_a = together(in_2, from_3, drive_a)
    out_2 = last_y + mm(last_t, in_2)
    base = first_x + mm(first_w, in_1 + in_2)
    outflow_2 = from_3[:, :k] + mm(from_3[:, k:], out_2)
    turn = base + mm(first_s, outflow_2)
    outflow_1 = send(turn, (2, 1))
    from_3, out_2, scale, _ = together(from_3, out_2, grain_scale, turn)
    in_3 = send(out_2, (2, 3))
    drive_b = drive(n // 2, n, me, scale, pivots, pieces)
    w_3 = from_3[:, k:]
    around = first_w + mm(first_s, mm(w_3, last_t))
    outflow_1, drive_b, around = together(outflow_1, drive_b, around)
    around = send(around, (2, 1))
    outflow_0 = send(base + mm(first_s, outflow_1), (1, 0))

    x_of_3, first_of_3 = second_of_3(
        places, lower, upper, x, high, low, drive_a, drive_b, probes, in_3
    )
    x_3 = send(first_of_3, (3, 2))
    outflow_0, x_of_3 = together(outflow_0, x_of_3)
    ahead, u, last_y = second_ahead(
        places, lower, upper, x, high, low, drive_a, drive_b,
        in_1, in_2, outflow_0, outflow_1, outflow_2,
    )

    in_1 = send(last_y, (0, 1))
    x, first_x = second_back(places, ahead, u, x_of_3)
    in_1, first_x, around = together(in_1, first_x, around)
    base = first_x + mm(first_s, mm(w_3, last_y))
    x_3, base = together(x_3, base)
    joined = jnp.where(domain == 1, last_y + mm(last_t, in_1), base + mm(first_s, x_3))
    swapped = send(joined, (1, 2), (2, 1))
    past = mm(around, joined)
    base = jnp.where(
        domain == 1, first_x + mm(first_w, in_1) + mm(first_s, past), last_y
    )
    across = jnp.where(domain == 1, first_s, last_t)
    swapped, base, across, past = together(swapped, base, across, past)
    crossing = base + mm(across, swapped)
    ended = send(crossing, (1, 0), (2, 3))
    beyond = x_3 + mm(w_3, crossing)

    weight = weights / (k * energies)
    terms = charge(places, weight, energies, x, high, low, probes, in_1, swapped, swapped + past, beyond, ended)
    summed = jnp.sum(lax.all_to_all(terms, "energy", 0, 0, tiled=True), axis=0)
    return summed[:, : b // energies]


def solution(mesh):
    placed = (
        P("energy", "dom", None, None),
        P("energy", "dom", None, None),
        P("energy", "dom", None, None),
        P("dom", "energy", None),
        P("dom"),
        P(),
        P("dom", None, None),
        P("energy"),
    )
    return jax.shard_map(
        per_device, mesh=mesh, in_specs=placed, out_specs=P("dom", "energy"), check_vma=False
    )
```

```python
import functools

import jax
import jax.numpy as jnp
from jax import lax
from jax.experimental import pallas as pl
from jax.experimental.pallas import tpu as pltpu
from jax.sharding import PartitionSpec as P

F32 = jnp.float32
BF16 = jnp.bfloat16
HIGH = lax.Precision.HIGH
MIB = 1 << 20


def halves(x):
    high = x.astype(BF16)
    return high, (x - high.astype(F32)).astype(BF16)


def dot(a, b):
    return jnp.dot(a, b, preferred_element_type=F32)


def left_two(a):
    return jnp.concatenate(halves(a), axis=1)


def left_three(a):
    high, low = halves(a)
    return jnp.concatenate([high, low, high], axis=1)


def apply_two(a, x):
    width = x.shape[1]
    both = jnp.concatenate(halves(x), axis=1)
    out = dot(a, jnp.concatenate([both, both], axis=0))
    return out[:, :width] + out[:, width:]


def apply_three(a, high, low):
    return dot(a, jnp.concatenate([high, high, low], axis=0))


def shapes(*entries):
    return [jax.ShapeDtypeStruct(shape, kind) for shape, kind in entries]


def cost(us):
    return pl.CostEstimate(flops=int(us * 1e9), bytes_accessed=0, transcendentals=0)


def params(mib):
    return pltpu.CompilerParams(vmem_limit_bytes=mib * MIB)


HBM = pl.BlockSpec(memory_space=pltpu.HBM)
VMEM = pl.BlockSpec(memory_space=pltpu.VMEM)
SMEM = pl.BlockSpec(memory_space=pltpu.SMEM)


def pinned(*entries):
    return [pltpu.VMEM(shape, kind) for shape, kind in entries]


def in_vmem(*arrays):
    return [pltpu.with_memory_space_constraint(x, pltpu.VMEM) for x in arrays]


def in_hbm(*arrays):
    return [pltpu.with_memory_space_constraint(x, pltpu.HBM) for x in arrays]


def local_kernel(
    pivot, lower, upper, probe,
    x_out, high_out, low_out, last_y, last_t, first_xw, first_x, first_w, first_s,
    d, l, u, z, left_a, left_b, given_a, given_b, h, x, high, low, sem, sem_out,
):
    n, b, k = z.shape
    kb = k + b
    wide = h.shape[2]
    lefts, givens = (left_a, left_b), (given_a, given_b)

    def load(which, i):
        src, dst = ((probe, z), (pivot, d), (lower, l), (upper, u))[which]
        return pltpu.make_async_copy(src.at[i], dst.at[i], sem.at[which, i])

    def store(which, i):
        src, dst = ((x, x_out), (high, high_out), (low, low_out))[which]
        return pltpu.make_async_copy(src.at[i], dst.at[i], sem_out.at[which, i])

    def begin(i, c):
        load(0, i).start()
        load(1, i).start()
        load(2, i).start()
        return c

    def begin_upper(i, c):
        load(3, n - 1 - i).start()
        return c

    lax.fori_loop(0, n, begin, 0)
    lax.fori_loop(0, n, begin_upper, 0)

    def arrive(i):
        load(0, i).wait()
        load(1, i).wait()
        load(2, i).wait()

    def prepare(i, slot):
        givens[slot][...] = apply_two(left_two(d[i]), z[i])
        lefts[slot][...] = left_three(l[i])

    def ahead(i, slot):
        moved = apply_three(lefts[slot][...], *halves(h[i - 1]))
        h[i, :, :k] = givens[slot][...] - moved[:, :k]
        h[i, :, k:] = -moved[:, k:]

    arrive(0)
    prepare(0, 0)
    h[0] = jnp.concatenate([given_a[...], -l[0], jnp.zeros((b, wide - kb), F32)], axis=1)
    arrive(1)
    prepare(1, 1)

    def ahead_pair(j, c):
        i = 2 * j + 1
        arrive(i + 1)
        ahead(i, 1)
        prepare(i + 1, 0)
        arrive(i + 2)
        ahead(i + 1, 0)
        prepare(i + 2, 1)
        return c

    lax.fori_loop(0, n // 2 - 1, ahead_pair, 0)

    def prepare_back(i, slot):
        lefts[slot][...] = left_three(u[i])

    def keep(i, value):
        value_high, value_low = halves(value)
        x[i] = value[:, :k]
        high[i] = value_high
        low[i] = value_low
        for which in range(3):
            store(which, i).start()

    def step_back(i, slot):
        moved = apply_three(lefts[slot][...], high[i + 1], low[i + 1])
        value = jnp.concatenate([h[i] - moved[:, :wide], -moved[:, wide:]], axis=1)
        keep(i, value)
        return value

    load(3, n - 1).wait()
    load(3, n - 2).wait()
    ahead(n - 1, 1)
    prepare_back(n - 1, 0)
    last_y[...] = h[n - 1, :, :k]
    last_t[...] = h[n - 1, :, k:kb]
    keep(n - 1, jnp.concatenate([h[n - 1, :, :kb], -u[n - 1]], axis=1))
    prepare_back(n - 2, 0)

    def back_pair(j, c):
        i = n - 2 - 2 * j
        load(3, i - 1).wait()
        step_back(i, 0)
        prepare_back(i - 1, 1)
        load(3, i - 2).wait()
        step_back(i - 1, 1)
        prepare_back(i - 2, 0)
        return c

    lax.fori_loop(0, n // 2 - 1, back_pair, 0)
    value = step_back(0, 0)
    first_xw[...] = value[:, :kb]
    first_x[...] = value[:, :k]
    first_w[...] = value[:, k:kb]
    first_s[...] = value[:, kb:]

    def drain(i, c):
        for which in range(3):
            store(which, i).wait()
        return c

    lax.fori_loop(0, n, drain, 0)


def local_maps(pivots, lower, upper, probes):
    n, b, k = probes.shape
    wide = -(-(k + b) // 128) * 128
    full = k + 2 * b
    v = pltpu.VMEM
    return pl.pallas_call(
        local_kernel,
        in_specs=[HBM] * 4,
        out_specs=[HBM] * 3 + [VMEM] * 6,
        out_shape=[
            pltpu.HBM((n, b, k), F32),
            pltpu.HBM((n, b, full), BF16),
            pltpu.HBM((n, b, full), BF16),
        ]
        + pinned(
            ((b, k), F32),
            ((b, b), F32),
            ((b, k + b), F32),
            ((b, k), F32),
            ((b, b), F32),
            ((b, b), F32),
        ),
        scratch_shapes=[
            v((n, b, b), F32),
            v((n, b, b), F32),
            v((n, b, b), F32),
            v((n, b, k), F32),
            v((b, 3 * b), BF16),
            v((b, 3 * b), BF16),
            v((b, k), F32),
            v((b, k), F32),
            v((n, b, wide), F32),
            v((n, b, k), F32),
            v((n, b, full), BF16),
            v((n, b, full), BF16),
            pltpu.SemaphoreType.DMA((4, n)),
            pltpu.SemaphoreType.DMA((3, n)),
        ],
        compiler_params=params(52),
        cost_estimate=cost(15),
        name="local_maps",
    )(*in_hbm(pivots, lower, upper, probes))


def drive_kernel(start, me, scale, pivot, *rest):
    pieces, out, gathered = rest[:-2], rest[-2], rest[-1]
    step = pl.program_id(0)
    for i in range(2):
        if len(pieces) > 1:
            rows = pieces[0].shape[1]
            for j, piece in enumerate(pieces):
                owner = lax.bitwise_xor(me[0], j)
                gathered[i, pl.ds(pl.multiple_of(owner * rows, 8), rows), :] = piece[i]
            potential = gathered[i]
        else:
            potential = pieces[0][i]
        potential = potential * scale[2 * step + i + start]
        out[2 * step + i] = left_two(apply_three(left_three(pivot[i]), *halves(potential)))


def drive(start, stop, me, scale, pivots, pieces):
    b = pivots.shape[1]
    rows = pieces[0].shape[1]
    at = lambda i: (i + start // 2, 0, 0)
    return pl.pallas_call(
        functools.partial(drive_kernel, start),
        grid=((stop - start) // 2,),
        in_specs=[SMEM, SMEM, pl.BlockSpec((2, b, b), at)]
        + [pl.BlockSpec((2, rows, b), at)] * len(pieces),
        out_specs=VMEM,
        out_shape=pltpu.VMEM((stop - start, b, 2 * b), BF16),
        scratch_shapes=[pltpu.VMEM((2, b, b), F32)],
        compiler_params=params(14),
        cost_estimate=cost(0.01),
        name="drive_maps",
    )(me, scale, *in_hbm(pivots, *pieces))


def add_flows(x, high, low, i, flows):
    n, b, k = x.shape
    skip = high.shape[2] - flows.shape[0]
    rows = lambda ref: ref[pl.ds(i, 2), :, skip:].reshape(2 * b, flows.shape[0])
    out = dot(rows(high), flows) + dot(rows(low), flows)
    out = out[:, :k] + out[:, k:]
    return x[i] + out[:b], x[i + 1] + out[b:]


def sweep_ahead(
    lower, upper, x, high, low, drive_a, drive_b, inflow, outflow, y, u, l, left_a, left_b, sem
):
    n, b, k = x.shape
    lefts = (left_a, left_b)
    load_l = lambda i: pltpu.make_async_copy(lower.at[i], l.at[i], sem.at[0, i])
    load_u = lambda i: pltpu.make_async_copy(upper.at[i], u.at[i], sem.at[1, i])

    def begin(i, c):
        load_l(i).start()
        load_u(i).start()
        return c

    lax.fori_loop(0, n, begin, 0)
    flows = jnp.concatenate(halves(jnp.concatenate([inflow, outflow], axis=0)), axis=1)
    half = drive_a.shape[0]
    for start, driver in ((0, drive_a), (half, drive_b)):

        def given(r, c):
            j = 2 * r
            i = j + start
            ahead_0, ahead_1 = add_flows(x, high, low, i, flows)
            y[i] = apply_two(driver[j], ahead_0)
            y[i + 1] = apply_two(driver[j + 1], ahead_1)
            return c

        lax.fori_loop(0, driver.shape[0] // 2, given, 0)

    def arrive(i, c):
        load_l(i).wait()
        load_u(i).wait()
        return c

    lax.fori_loop(0, n, arrive, 0)
    left_b[...] = left_two(l[1])

    def step(i, slot):
        y[i] = y[i] - apply_two(lefts[slot][...], y[i - 1])

    def pair(j, c):
        i = 2 * j + 1
        step(i, 1)
        left_a[...] = left_two(l[i + 1])
        step(i + 1, 0)
        left_b[...] = left_two(l[i + 2])
        return c

    lax.fori_loop(0, n // 2 - 1, pair, 0)
    step(n - 1, 1)


def sweep_back(y, u, x_out, out, left_a, left_b, sem):
    n = y.shape[0]
    lefts = (left_a, left_b)
    store = lambda i: pltpu.make_async_copy(out.at[i], x_out.at[i], sem.at[i])
    left_a[...] = left_two(u[n - 2])
    out[n - 1] = y[n - 1]
    store(n - 1).start()

    def step(i, slot):
        out[i] = y[i] - apply_two(lefts[slot][...], out[i + 1])
        store(i).start()

    def pair(j, c):
        i = n - 2 - 2 * j
        step(i, 0)
        left_b[...] = left_two(u[i - 1])
        step(i - 1, 1)
        left_a[...] = left_two(u[i - 2])
        return c

    lax.fori_loop(0, n // 2 - 1, pair, 0)
    step(0, 0)

    def drain(i, c):
        store(i).wait()
        return c

    lax.fori_loop(0, n, drain, 0)


def second_of_3_kernel(
    places, lower, upper, x, high, low, drive_a, drive_b, probes, in_3,
    x_out, first, y, u, out, l, left_a, left_b, sem, sem_out,
):
    @pl.when(places[0] == 3)
    def _():
        inflow = in_3[...]
        sweep_ahead(
            lower, upper, x, high, low, drive_a, drive_b, inflow, jnp.zeros_like(inflow),
            y, u, l, left_a, left_b, sem,
        )
        sweep_back(y, u, x_out, out, left_a, left_b, sem_out)
        first[...] = out[0]

    @pl.when(places[0] != 3)
    def _():
        first[...] = jnp.zeros_like(first)


def second_of_3(places, lower, upper, x, high, low, drive_a, drive_b, probes, in_3):
    n, b, k = x.shape
    v = pltpu.VMEM
    return pl.pallas_call(
        second_of_3_kernel,
        in_specs=[SMEM] + [HBM] * 2 + [VMEM] * 7,
        out_specs=[HBM, VMEM],
        out_shape=[pltpu.HBM((n, b, k), F32), pltpu.VMEM((b, k), F32)],
        scratch_shapes=[
            v((n, b, k), F32),
            v((n, b, b), F32),
            v((n, b, k), F32),
            v((n, b, b), F32),
            v((b, 2 * b), BF16),
            v((b, 2 * b), BF16),
            pltpu.SemaphoreType.DMA((2, n)),
            pltpu.SemaphoreType.DMA((n,)),
        ],
        compiler_params=params(18),
        cost_estimate=cost(0.01),
        name="second_of_3",
    )(places, *in_hbm(lower, upper), *in_vmem(x, high, low, drive_a, drive_b, probes), in_3)


def second_ahead_kernel(
    lower, upper, x, high, low, drive_a, drive_b, in_1, in_2, out_0, out_1, out_2,
    y, u, last, l, left_a, left_b, sem,
):
    inflow = in_1[...] + in_2[...]
    outflow = out_0[...] + out_1[...] + out_2[...]
    sweep_ahead(
        lower, upper, x, high, low, drive_a, drive_b, inflow, outflow,
        y, u, l, left_a, left_b, sem,
    )
    last[...] = y[y.shape[0] - 1]


def second_ahead(lower, upper, x, high, low, drive_a, drive_b, *flows):
    n, b, k = x.shape
    return pl.pallas_call(
        second_ahead_kernel,
        in_specs=[HBM] * 2 + [VMEM] * (5 + len(flows)),
        out_specs=[VMEM] * 3,
        out_shape=pinned(((n, b, k), F32), ((n, b, b), F32), ((b, k), F32)),
        scratch_shapes=[
            pltpu.VMEM((n, b, b), F32),
            pltpu.VMEM((b, 2 * b), BF16),
            pltpu.VMEM((b, 2 * b), BF16),
            pltpu.SemaphoreType.DMA((2, n)),
        ],
        compiler_params=params(12),
        cost_estimate=cost(0.01),
        name="second_ahead",
    )(*in_hbm(lower, upper), *in_vmem(x, high, low, drive_a, drive_b), *flows)


def second_back_kernel(places, y, u, x_of_3, x_out, first, out, left_a, left_b, sem):
    @pl.when(places[0] != 3)
    def _():
        sweep_back(y, u, x_out, out, left_a, left_b, sem)
        first[...] = out[0]

    @pl.when(places[0] == 3)
    def _():
        first[...] = jnp.zeros_like(first)


def second_back(places, y, u, x_of_3):
    n, b, k = y.shape
    return pl.pallas_call(
        second_back_kernel,
        in_specs=[SMEM] + [VMEM] * 2 + [HBM],
        out_specs=[HBM, VMEM],
        out_shape=[pltpu.HBM((n, b, k), F32), pltpu.VMEM((b, k), F32)],
        input_output_aliases={3: 0},
        scratch_shapes=[
            pltpu.VMEM((n, b, k), F32),
            pltpu.VMEM((b, 2 * b), BF16),
            pltpu.VMEM((b, 2 * b), BF16),
            pltpu.SemaphoreType.DMA((n,)),
        ],
        compiler_params=params(5),
        cost_estimate=cost(0.01),
        name="second_back",
    )(places, *in_vmem(y, u), *in_hbm(x_of_3))


def charge_kernel(places, weight, x, high, low, probe, in_1, in_2, out_1, out_2, ended, blocks, terms):
    n, b, k = x.shape
    at = places[0]
    none = jnp.zeros_like(ended)
    inflow = jnp.where(at == 1, in_1[...], jnp.where(at == 2, in_2[...], none))
    inflow = jnp.where(at == 3, ended[...], inflow)
    outflow = jnp.where(at == 1, out_1[...], jnp.where(at == 2, out_2[...], none))
    outflow = jnp.where(at == 0, ended[...], outflow)
    flows = jnp.concatenate(halves(jnp.concatenate([inflow, outflow], axis=0)), axis=1)
    skip = high.shape[2] - flows.shape[0]
    for i in range(n):
        maps = jnp.concatenate([high[i, :, skip:], low[i, :, skip:]], axis=1)
        out = dot(maps, jnp.concatenate([flows, flows], axis=0))
        value = x[i] + out[:, :k] + out[:, k:]
        terms[i : i + 1, :] = jnp.sum((value * probe[i]).T, axis=0, keepdims=True) * weight[0]
    owners = blocks.shape[0]
    rows = b // owners
    for owner in range(owners):
        blocks[owner, :, :rows] = terms[:, owner * rows : (owner + 1) * rows]


def charge(places, weight, energies, x, high, low, probes, *flows):
    n, b, k = probes.shape
    wide = -(-(b // energies) // 128) * 128
    return pl.pallas_call(
        charge_kernel,
        in_specs=[SMEM] * 2 + [VMEM] * (4 + len(flows)),
        out_specs=VMEM,
        out_shape=pltpu.VMEM((energies, n, wide), F32),
        scratch_shapes=[pltpu.VMEM((n, b), F32)],
        compiler_params=params(10),
        name="charge_terms",
    )(places, weight, *in_vmem(x, high, low, probes), *flows)


def mm(a, b):
    return jnp.dot(a, b, precision=HIGH)


def send(x, *pairs):
    return lax.ppermute(x, "dom", list(pairs))


def near(x, ways):
    peers = lax.axis_size("energy")
    return [lax.ppermute(x, "energy", [(i, i ^ way) for i in range(peers)]) for way in ways]


def together(*values):
    return lax.optimization_barrier(values)


def per_device(
    pivots, lower_spikes, upper_spikes, potential, grain_of_slice, grain_shift, probes, weights
):
    pivots, lower, upper = pivots[0], lower_spikes[0], upper_spikes[0]
    k = probes.shape[2]
    energies = lax.axis_size("energy")
    me = lax.axis_index("energy").astype(jnp.int32).reshape(1)
    domain = lax.axis_index("dom")
    grain_count = grain_shift.shape[0]
    grain_match = grain_of_slice[:, None] == jnp.arange(grain_count, dtype=jnp.int32)[None, :]
    grain_scale = jnp.sum(jnp.where(grain_match, grain_shift[None, :], 0.0), axis=1)
    by_swaps = energies == 8 and potential.shape[1] % 8 == 0

    places = jnp.stack([domain, lax.axis_index("energy")]).astype(jnp.int32)
    n, b = pivots.shape[:2]

    even = near(potential, (2, 4, 6)) if by_swaps else []
    x, high, low, last_y, last_t, first_xw, first_x, first_w, first_s = local_maps(
        pivots, lower, upper, probes
    )

    if by_swaps:
        last_y, even[0] = together(last_y, even[0])
    in_1 = send(last_y, (0, 1))
    from_3 = send(first_xw, (3, 2))
    if by_swaps:
        in_1, even[1], even[2] = together(in_1, even[1], even[2])
    out_1 = last_y + mm(last_t, in_1)
    in_2 = send(out_1, (1, 2))
    if by_swaps:
        even = [potential] + even
        odd = [near(block, (1,))[0] for block in even]
        pieces = [block for pair in zip(even, odd) for block in pair]
    else:
        pieces = [lax.all_gather(potential, "energy", axis=1, tiled=True)]
    drive_a = drive(0, n // 2, me, grain_scale, pivots, pieces)
    in_2, from_3, drive_a = together(in_2, from_3, drive_a)
    out_2 = last_y + mm(last_t, in_2)
    base = first_x + mm(first_w, in_1 + in_2)
    outflow_2 = from_3[:, :k] + mm(from_3[:, k:], out_2)
    turn = base + mm(first_s, outflow_2)
    outflow_1 = send(turn, (2, 1))
    from_3, out_2, scale, _ = together(from_3, out_2, grain_scale, turn)
    in_3 = send(out_2, (2, 3))
    drive_b = drive(n // 2, n, me, scale, pivots, pieces)
    w_3 = from_3[:, k:]
    around = first_w + mm(first_s, mm(w_3, last_t))
    outflow_1, drive_b, around = together(outflow_1, drive_b, around)
    around = send(around, (2, 1))
    outflow_0 = send(base + mm(first_s, outflow_1), (1, 0))

    x_of_3, first_of_3 = second_of_3(
        places, lower, upper, x, high, low, drive_a, drive_b, probes, in_3
    )
    x_3 = send(first_of_3, (3, 2))
    outflow_0, x_of_3 = together(outflow_0, x_of_3)
    ahead, u, last_y = second_ahead(
        lower, upper, x, high, low, drive_a, drive_b,
        in_1, in_2, outflow_0, outflow_1, outflow_2,
    )

    in_1 = send(last_y, (0, 1))
    x, first_x = second_back(places, ahead, u, x_of_3)
    in_1, first_x, around = together(in_1, first_x, around)
    base = first_x + mm(first_s, mm(w_3, last_y))
    x_3, base = together(x_3, base)
    joined = jnp.where(domain == 1, last_y + mm(last_t, in_1), base + mm(first_s, x_3))
    swapped = send(joined, (1, 2), (2, 1))
    past = mm(around, joined)
    base = jnp.where(
        domain == 1, first_x + mm(first_w, in_1) + mm(first_s, past), last_y
    )
    across = jnp.where(domain == 1, first_s, last_t)
    swapped, base, across, past = together(swapped, base, across, past)
    crossing = base + mm(across, swapped)
    ended = send(crossing, (1, 0), (2, 3))
    beyond = x_3 + mm(w_3, crossing)

    weight = weights / (k * energies)
    terms = charge(places, weight, energies, x, high, low, probes, in_1, swapped, swapped + past, beyond, ended)
    summed = jnp.sum(lax.all_to_all(terms, "energy", 0, 0, tiled=True), axis=0)
    return summed[:, : b // energies]


def solution(mesh):
    placed = (
        P("energy", "dom", None, None),
        P("energy", "dom", None, None),
        P("energy", "dom", None, None),
        P("dom", "energy", None),
        P("dom"),
        P(),
        P("dom", None, None),
        P("energy"),
    )
    return jax.shard_map(
        per_device, mesh=mesh, in_specs=placed, out_specs=P("dom", "energy"), check_vma=False
    )
```
